32 devices in a mesh: tm: 4 (over z), lat: 4 (over y, x), lon: 2 (over core).
Axes of the slice: x: 2, y: 2, z: 4, core: 2. Of those that a mesh axis runs over, the one named last changes fastest.
Arguments:
- slab: bfloat16 [512, 65536], P('tm', ('lat', 'lon')), may hold values from -6 to 6
- start: bfloat16 [512, 64], P('tm'), may hold values from -6 to 6
- sections: float32 [3, 2], replicated, may hold values from 0.2 to 1.5708, as said below
Outputs:
- basis: float32 [512, 64, 128], P(('lat', 'lon', 'tm'))
- pcs: float32 [512, 64], P('tm')
The draws below stay inside these ranges and needn't reach their ends.
Inputs may be any that keep to these rules, and one draw needn't show every extreme that they name: `sections`: in each column, one section has radius 0.78 to 0.86 and angle 2 pi / 8 to 2 pi / 4, the other radius 0.9955 to 0.9985 and angle 2 pi / 24 to 2 pi / 12; which column is which varies; amplitudes 0.2 to 1.0.
All inputs are finite; a program needn't handle non-finite values.
Results may differ from the reference program's by a relative error of at most 0.0039.
Values may be sent and summed in bfloat16 or wider, within the bound.
No kernel may reach another device: no remote copies, remote signals or barrier semaphores. Data moves between devices by JAX's collectives and lax.ppermute only.
A program may use at most 64 MiB of HBM per device.

```python
import math
import jax
import jax.numpy as jnp
from jax import lax

HOURS = 512
K = 64
LANES = 128
CELLS = 65536
GROUPS = 512


def draw_sections(key, part):
    picks = jax.random.uniform(key, (3, 2), jnp.float32)
    broad = jnp.stack([0.78 + 0.08 * picks[0, 0], 2.0 * math.pi / (4.0 + 4.0 * picks[1, 0]), 0.6 + 0.4 * picks[2, 0]])
    slower = jnp.stack([0.9955 + 0.003 * picks[0, 1], 2.0 * math.pi / (12.0 + 12.0 * picks[1, 1]), 0.2 + 0.15 * picks[2, 1]])
    flipped = jax.random.randint(jax.random.fold_in(key, 7), (), 0, 2)
    first_column = jnp.where(flipped == 0, broad, slower)
    second_column = jnp.where(flipped == 0, slower, broad)
    return jnp.stack([first_column, second_column], axis=1).astype(jnp.float32)


def shard_levels(key, dims, split, low, top_value):
    gain, own = 1.0, jax.random.fold_in(key, 6)
    for position, shards_of in split:
        heights = jnp.exp(jax.random.uniform(jax.random.fold_in(own, position), (shards_of,), jnp.float32, low / len(split), top_value / len(split)))
        gain = gain * jnp.repeat(heights, dims[position] // shards_of).reshape([-1 if axis == position else 1 for axis in range(len(dims))])
    return gain


def gaussian(rng, shape, deviation, most, split=(), held_as=jnp.bfloat16):
    values = deviation * jax.random.normal(rng, shape, jnp.float32)
    if split:
        values = values * shard_levels(rng, shape, split, -0.22, 0.18)
    return jnp.clip(values, -most, most).astype(held_as)


def setup_inputs(seed: int = 0) -> dict:
    key_of = jax.random.split(jax.random.key(seed), 4)
    slab = gaussian(key_of[0], (HOURS, CELLS), 1.0, 6.0, ((0, 4), (1, 8)))
    start = gaussian(key_of[1], (HOURS, K), 1.0, 6.0, ((0, 4),))
    sections = draw_sections(jax.random.fold_in(key_of[3], 71), 0)
    return {"slab": slab, "start": start, "sections": sections}


def filter_rows(sections):
    radius = sections[0]
    angles = sections[1]
    amplitude = sections[2]
    feed_one = 2.0 * radius * jnp.cos(angles)
    feed_two = -radius * radius
    drive_gain = amplitude * jnp.sqrt(1.0 - radius * radius)
    return (feed_one, feed_two, drive_gain)

def advance(carried, inputs, coefficients):
    feed_one, feed_two, drive_gain = coefficients
    residual_gap = inputs - carried[1]
    section_one = drive_gain[0] * residual_gap + feed_one[0] * carried[2] + feed_two[0] * carried[3]
    section_two = drive_gain[1] * residual_gap + feed_one[1] * carried[4] + feed_two[1] * carried[5]
    updated = jnp.stack([inputs, carried[0], section_one, carried[2], section_two, carried[4]])
    return (updated, section_one + section_two)

def reference(slab, start, sections):
    coefficients = filter_rows(sections)
    cell_count = slab.shape[1]

    def hour_step(carried, row_values):
        updated, output = advance(carried, row_values.astype(jnp.float32), coefficients)
        return (updated, output.astype(jnp.bfloat16))
    initial = jnp.zeros((6, cell_count), jnp.float32)
    _, filtered = lax.scan(hour_step, initial, slab)
    spatial_patterns = jnp.dot(start.T.astype(jnp.float32), filtered.astype(jnp.float32), preferred_element_type=jnp.float32)
    gram_matrix = jnp.dot(spatial_patterns, spatial_patterns.T, precision=lax.Precision.HIGHEST)
    lower_factor = jnp.linalg.cholesky(gram_matrix)
    inverse_factor = jax.scipy.linalg.solve_triangular(lower_factor, jnp.eye(K, dtype=jnp.float32), lower=True)
    ortho = jnp.dot(inverse_factor, spatial_patterns, precision=lax.Precision.HIGHEST)
    basis = (ortho * math.sqrt(CELLS)).reshape(K, GROUPS, LANES).transpose(1, 0, 2)

    def project_block(block_of_rows):
        return jnp.dot(block_of_rows.astype(jnp.float32), ortho.T, precision=lax.Precision.HIGHEST)
    blocks = filtered.reshape(8, HOURS // 8, CELLS)
    pcs = lax.map(project_block, blocks).reshape(HOURS, K) * math.sqrt(HOURS / CELLS)
    return (basis, pcs)
```

```python
import functools
import math

import jax
import jax.numpy as jnp
from jax import lax
from jax.experimental import pallas as pl
from jax.experimental.pallas import tpu as pltpu
from jax.sharding import PartitionSpec as P

LANES = 128
STATES = 8
TOP = lax.Precision.HIGHEST
VMEM_LIMIT = 24 * 1024 * 1024


def tables(sections, hours):
    radius, angle, amplitude = sections
    drive = amplitude * jnp.sqrt(1.0 - radius * radius)
    back = 1.0 / (radius * radius)
    gain_re = drive * (1.0 + back)
    gain_im = -drive * (1.0 - back) * jnp.cos(angle) / jnp.sin(angle)
    log_radius = jnp.log(radius)
    hour = jnp.arange(hours, dtype=jnp.float32)

    def power(n):
        size = jnp.exp(n[None, :] * log_radius[:, None])
        turn = n[None, :] * angle[:, None]
        return size * jnp.cos(turn), size * jnp.sin(turn)

    def rows(real, imag):
        four = jnp.stack([real[0], imag[0], real[1], imag[1]])
        return jnp.concatenate([four, four])

    re, im = power(hour)
    outgoing = rows(
        gain_re[:, None] * re - gain_im[:, None] * im,
        -(gain_re[:, None] * im + gain_im[:, None] * re),
    )
    inverse = rows(*power(-hour))
    incoming = rows(*power(hours - hour))
    lam_re, lam_im = power(jnp.full((LANES,), hours, jnp.float32))
    keep = rows(lam_re, lam_re)
    swap = rows(-lam_im, lam_im)
    diagonal = jnp.broadcast_to(jnp.sum(drive), (STATES, LANES))
    return outgoing, outgoing.T, incoming, inverse, keep, swap, diagonal


def doubled(value):
    rounded = value.astype(jnp.bfloat16).astype(jnp.float32)
    row = lax.broadcasted_iota(jnp.int32, value.shape, 0)
    return jnp.where(row < STATES // 2, rounded, value - rounded)


def joined(value):
    return value + pltpu.roll(value, STATES // 2, 0)


def advanced(value, keep, swap):
    row = lax.broadcasted_iota(jnp.int32, value.shape, 0)
    other = jnp.where(row % 2 == 0, pltpu.roll(value, STATES - 1, 0), pltpu.roll(value, 1, 0))
    return keep * value + swap * other


def outer(columns, rows):
    total = columns[:, 0:1] * rows[0:1, :]
    for k in range(1, STATES // 2):
        total = total + columns[:, k : k + 1] * rows[k : k + 1, :]
    return total


def head_kernel(parts, left_ref, slab_ref, start_ref, out_ref, col_ref, in_ref, inv_ref, diag_ref, *results):
    sums, messages = results[:parts], results[parts : 2 * parts]
    filter_ref, wcol_ref, wrow_ref = results[2 * parts :]
    hours, width = start_ref.shape
    left = left_ref[0] != 0
    later = lax.broadcasted_iota(jnp.int32, (hours, hours), 0)
    earlier = lax.broadcasted_iota(jnp.int32, (hours, hours), 1)
    full = outer(col_ref[...], inv_ref[...])
    full = jnp.where(later > earlier, full, jnp.where(later == earlier, diag_ref[0:1, 0:1], 0.0))
    filter_ref[...] = full
    start = start_ref[...].astype(jnp.float32)
    over_hours = (((0,), (0,)), ((), ()))
    weights = lax.dot_general(start, full, over_hours, precision=TOP)
    wcol_ref[...] = lax.dot_general(start, col_ref[...], over_hours, precision=TOP)
    wrow = jnp.dot(out_ref[...], start, precision=TOP)
    wrow_ref[...] = jnp.concatenate([wrow, jnp.zeros((STATES, LANES - width), jnp.float32)], axis=1)
    weights = jnp.concatenate([weights, in_ref[...]], axis=0)
    high = weights.astype(jnp.bfloat16)
    low = (weights - high.astype(jnp.float32)).astype(jnp.bfloat16)
    offset = 0
    for part in range(parts):
        cells = sums[part].shape[1]
        block = slab_ref[:, offset : offset + cells]
        total = jnp.dot(high, block, preferred_element_type=jnp.float32) + jnp.dot(
            low, block, preferred_element_type=jnp.float32
        )
        sums[part][...] = total
        own = jnp.concatenate([wrow_ref[...], jnp.zeros((STATES, cells - LANES), jnp.float32)], axis=1)
        extra = doubled(jnp.where(left, total[width:], own))
        messages[part][...] = jnp.concatenate([total[:width], extra], axis=0).astype(jnp.bfloat16)
        offset += cells


def column_of(rows, width):
    return jnp.transpose(rows[:, :LANES])[:width]


def inward_kernel(left_ref, recv_ref, sum_ref, wcol_ref, wrow_ref, keep_ref, swap_ref, total_ref, message_ref):
    width = wcol_ref.shape[0]
    left = left_ref[0] != 0
    cells = sum_ref.shape[1]
    received = recv_ref[...].astype(jnp.float32)
    states = joined(received[width:])
    own = sum_ref[...]
    columns = jnp.where(left, wcol_ref[...], column_of(states, width))
    rows = jnp.where(left, states, own[width:])
    total = received[:width] + own[:width] + outer(columns, rows)
    padded = jnp.concatenate([wrow_ref[...], jnp.zeros((STATES, cells - LANES), jnp.float32)], axis=1)
    swap = jnp.where(left, swap_ref[:, 0:1], -swap_ref[:, 0:1])
    extra = advanced(states, keep_ref[:, 0:1], swap) + jnp.where(left, own[width:], padded)
    total_ref[...] = jnp.concatenate([total, extra], axis=0)
    message_ref[...] = jnp.concatenate([total, doubled(extra)], axis=0).astype(jnp.bfloat16)


def middle_kernel(left_ref, recv_ref, own_ref, sum_ref, keep_ref, swap_ref, total_ref, message_ref):
    width = total_ref.shape[0]
    left = left_ref[0] != 0
    received = recv_ref[...].astype(jnp.float32)
    states = joined(received[width:])
    own = own_ref[...]
    columns = column_of(jnp.where(left, states[:, :LANES], own[width:, :LANES]), width)
    rows = jnp.where(left, own[width:], states)
    total = received[:width] + own[:width] + outer(columns, rows)
    total_ref[...] = total
    extra = advanced(states, keep_ref[:, 0:1], swap_ref[:, 0:1]) + sum_ref[width:, :]
    message_ref[...] = jnp.concatenate([total, doubled(extra)], axis=0).astype(jnp.bfloat16)


def gather_kernel(middle, first, pick_ref, slab_ref, total_ref, *refs):
    refs = list(refs)
    kept_ref, sums_ref = refs[-2:]
    before_ref = None if first else refs.pop(0)
    received = [ref[...].astype(jnp.float32) for ref in refs[:-2]]
    width = total_ref.shape[0]
    hours = slab_ref.shape[0]
    total = jnp.where(pick_ref[len(received)] != 0, total_ref[...], 0.0)
    for block in received[middle + 1 :]:
        total = total + block[:width]
    states = jnp.zeros_like(received[0][width:])
    for place, block in enumerate(received):
        states = states + jnp.where(pick_ref[place] != 0, block[width:], 0.0)
    kept_ref[...] = total
    patterns = total.astype(jnp.bfloat16)

    def product(value):
        return lax.dot_general(value, patterns, (((1,), (1,)), ((), ())), preferred_element_type=jnp.float32)

    blocks = (product(slab_ref[...]), product(patterns), product(states.astype(jnp.bfloat16)))
    spans = ((0, hours), (hours, hours + width), (hours + width, hours + width + STATES))
    for (low, high), block in zip(spans, blocks):
        sums_ref[low:high, :] = block if first else before_ref[low:high, :] + block


def inverse_factor(gram):
    width = gram.shape[0]
    row = lax.broadcasted_iota(jnp.int32, (width, width), 0)
    column = lax.broadcasted_iota(jnp.int32, (width, width), 1)
    work = jnp.concatenate([gram, jnp.where(row == column, 1.0, 0.0)], axis=1)
    index = lax.broadcasted_iota(jnp.int32, (width, 1), 0)
    for k in range(width - 1):
        pivot = work[k : k + 1, :]
        factor = jnp.where(index > k, work[:, k : k + 1] / pivot[:, k : k + 1], 0.0)
        work = work - factor * pivot
    diagonal = jnp.sum(jnp.where(row == column, work[:, :width], 0.0), axis=1, keepdims=True)
    return work[:, width:] * lax.rsqrt(diagonal)


def tail_kernel(basis_scale, pcs_scale, one_ref, two_ref, filter_ref, col_ref, own_ref, basis_ref, pcs_ref):
    hours = filter_ref.shape[0]
    width = own_ref.shape[0]
    sums = one_ref[...] + two_ref[...]
    inverse = inverse_factor(sums[hours : hours + width])
    states = joined(sums[hours + width :])
    filtered = jnp.dot(filter_ref[...], sums[:hours], precision=TOP) + outer(col_ref[...], states)
    pcs_ref[...] = lax.dot_general(
        filtered, inverse * pcs_scale, (((1,), (1,)), ((), ())), precision=TOP
    )
    basis = jnp.dot(inverse * basis_scale, own_ref[...], precision=TOP)
    for group in range(basis_ref.shape[0]):
        basis_ref[group] = basis[:, group * LANES : (group + 1) * LANES]


def call(kernel, name, out_shape, *args, scalars=1, **kwargs):
    smem = pl.BlockSpec(memory_space=pltpu.SMEM)
    vmem = pl.BlockSpec(memory_space=pltpu.VMEM)
    return pl.pallas_call(
        kernel,
        out_shape=out_shape,
        in_specs=kwargs.pop("in_specs", [smem] * scalars + [vmem] * (len(args) - scalars)),
        out_specs=jax.tree.map(lambda _: vmem, out_shape),
        compiler_params=pltpu.CompilerParams(vmem_limit_bytes=VMEM_LIMIT),
        name=name,
    )(*args)


def local(slab, start, sections):
    hours, cells = slab.shape
    width = start.shape[1]
    line = lax.axis_size("tm")
    place = lax.axis_index("tm")
    half = line // 2
    parts = 4
    part_cells = cells // parts
    tall = width + STATES
    f32, bf16 = jnp.float32, jnp.bfloat16
    shape = jax.ShapeDtypeStruct

    outgoing, columns, incoming, inverse, keep, swap, diagonal = tables(sections, hours)
    left = (place < half).astype(jnp.int32).reshape(1)
    results = call(
        functools.partial(head_kernel, parts),
        "head",
        [shape((tall, part_cells), f32)] * parts
        + [shape((tall, part_cells), bf16)] * parts
        + [shape((hours, hours), f32), shape((width, STATES), f32), shape((STATES, LANES), f32)],
        left, slab, start, outgoing, columns, incoming, inverse, diagonal,
    )
    sums, messages = results[:parts], results[parts : 2 * parts]
    filter_rows, wcol, wrow = results[2 * parts :]

    picks = [place == hop + 1 for hop in range(half - 1)] + [place == half]
    picks += [place == half + 1 + hop for hop in range(half - 1)]
    picks += [(place == half - 1) | (place == half)]
    pick = jnp.stack(picks).astype(jnp.int32)

    pair = [shape((tall, part_cells), f32), shape((tall, part_cells), bf16)]
    kept, running = [], None
    for part in range(parts):
        message, total = messages[part], sums[part]
        received = []
        for hop in range(half - 1):
            moves = [(hop, hop + 1), (line - 1 - hop, line - 2 - hop)]
            block = lax.ppermute(message, "tm", moves)
            received.append(block)
            newer = call(inward_kernel, "inward", pair, left, block, sums[part], wcol, wrow, keep, swap)
            if half == 2:
                total, message = newer
            else:
                active = (place == hop + 1) | (place == line - 2 - hop)
                total, message = (jnp.where(active, new, old) for new, old in zip(newer, (total, message)))
        block = lax.ppermute(message, "tm", [(half - 1, half), (half, half - 1)])
        received.append(block)
        total, message = call(
            middle_kernel, "middle", [shape((width, part_cells), f32), pair[1]],
            left, block, total, sums[part], keep, swap,
        )
        for hop in range(half - 1):
            moves = [(half - 1 - hop, half - 2 - hop), (half + hop, half + 1 + hop)]
            block = lax.ppermute(message, "tm", moves)
            received.append(block)
            if hop < half - 2:
                active = (place == half - 2 - hop) | (place == half + 1 + hop)
                states = block[width:].astype(f32)
                states = states + jnp.roll(states, STATES // 2, 0)
                swapped = states.reshape(STATES // 2, 2, -1)[:, ::-1].reshape(states.shape)
                states = keep[:, :1] * states + swap[:, :1] * swapped + sums[part][width:]
                rounded = states.astype(bf16)
                rest = (states - rounded.astype(f32)).astype(bf16)
                forward = jnp.concatenate(
                    [block[:width], rounded[: STATES // 2], rest[STATES // 2 :]], axis=0
                )
                message = jnp.where(active, forward, message)
        before = [] if running is None else [running]
        smem, vmem = pl.BlockSpec(memory_space=pltpu.SMEM), pl.BlockSpec(memory_space=pltpu.VMEM)
        piece, running = call(
            functools.partial(gather_kernel, half - 1, running is None), "gather",
            [shape((width, part_cells), f32), shape((hours + width + STATES, width), f32)],
            pick, slab[:, part * part_cells : (part + 1) * part_cells], total, *before, *received,
        )
        kept.append(piece)

    steps = []
    for axis in ("lon", "lat"):
        size, stride = lax.axis_size(axis), 1
        while stride < size:
            steps.append((axis, [(i, i ^ stride) for i in range(size)]))
            stride *= 2
    for axis, moves in steps[:-1]:
        running = running + lax.ppermute(running, axis, moves)
    other = lax.ppermute(running, *steps[-1])

    cells_all = cells * lax.axis_size("lat") * lax.axis_size("lon")
    own_cells = cells // line
    own = lax.dynamic_slice_in_dim(jnp.concatenate(kept, axis=1), place * own_cells, own_cells, axis=1)
    basis, pcs = call(
        functools.partial(tail_kernel, math.sqrt(cells_all), math.sqrt(hours * line / cells_all)), "tail",
        [shape((own_cells // LANES, width, LANES), f32), shape((hours, width), f32)],
        running, other, filter_rows, columns, own, scalars=0,
    )
    return (basis, pcs)


def solution(mesh):
    return jax.shard_map(
        local,
        mesh=mesh,
        in_specs=(P("tm", ("lat", "lon")), P("tm", None), P()),
        out_specs=(P(("lat", "lon", "tm"), None, None), P("tm", None)),
        check_vma=False,
    )
```

```python
import functools
import math

import jax
import jax.numpy as jnp
from jax import lax
from jax.experimental import pallas as pl
from jax.experimental.pallas import tpu as pltpu
from jax.sharding import PartitionSpec as P

LANES = 128
STATES = 8
TOP = lax.Precision.HIGHEST
VMEM_LIMIT = 8 * 1024 * 1024


def row_pairs(first, second):
    row = lax.broadcasted_iota(jnp.int32, (STATES, LANES), 0)
    return jnp.where(row % 4 < 2, first, second)


def swapped(value):
    row = lax.broadcasted_iota(jnp.int32, value.shape, 0)
    return jnp.where(row % 2 == 0, pltpu.roll(value, STATES - 1, 0), pltpu.roll(value, 1, 0))


def tables(section_ref, hours):
    shape = (STATES, LANES)
    radius, angle, amplitude = (row_pairs(section_ref[0, i], section_ref[1, i]) for i in range(3))
    hour = lax.broadcasted_iota(jnp.int32, shape, 1).astype(jnp.float32)
    imaginary = lax.broadcasted_iota(jnp.int32, shape, 0) % 2 == 1
    sign = jnp.where(imaginary, 1.0, -1.0)
    drive = amplitude * jnp.sqrt(1.0 - radius * radius)
    back = 1.0 / (radius * radius)
    gain_re = drive * (1.0 + back)
    gain_im = -drive * (1.0 - back) * jnp.cos(angle) / jnp.sin(angle)
    log_radius = jnp.log(radius)

    def power(n):
        turn = n * angle
        return jnp.exp(n * log_radius) * jnp.where(imaginary, jnp.sin(turn), jnp.cos(turn))

    ahead = power(hour)
    outgoing = -sign * (gain_re * ahead + sign * gain_im * swapped(ahead))
    inverse, incoming = power(-hour), power(hours - hour)
    lam = power(jnp.full(shape, hours, jnp.float32))
    keep = jnp.where(imaginary, swapped(lam), lam)
    swap = sign * jnp.where(imaginary, lam, swapped(lam))
    diagonal = drive[0:1, 0:1] + drive[2:3, 0:1]
    return outgoing, incoming, inverse, keep, swap, diagonal


def doubled(value):
    rounded = value.astype(jnp.bfloat16).astype(jnp.float32)
    row = lax.broadcasted_iota(jnp.int32, value.shape, 0)
    return jnp.where(row < STATES // 2, rounded, value - rounded)


def joined(value):
    return value + pltpu.roll(value, STATES // 2, 0)


def advanced(value, keep, swap):
    return keep * value + swap * swapped(value)


def outer(columns, rows):
    total = columns[:, 0:1] * rows[0:1, :]
    for k in range(1, STATES // 2):
        total = total + columns[:, k : k + 1] * rows[k : k + 1, :]
    return total


class Layout:
    def __init__(self, hours, cells, width, parts):
        self.hours, self.width, self.parts, self.cells = hours, width, parts, cells
        self.part_cells = cells // parts
        self.own = slice(width, width + STATES)
        self.out = slice(width + STATES, width + 2 * STATES)
        self.enter = slice(width + 2 * STATES, width + 3 * STATES)
        self.blocks = hours // width
        self.filter = cells
        self.table = cells + self.blocks * LANES
        self.running = self.table + LANES
        self.columns = self.running + LANES * (-(-(hours + width + STATES) // LANES))
        self.shape = (width + 3 * STATES, self.columns)

    def part(self, part):
        return slice(part * self.part_cells, (part + 1) * self.part_cells)

    def rows(self, work, place):
        return work[place * STATES : (place + 1) * STATES, self.table : self.table + LANES]

    def filter_block(self, block):
        start = self.filter + block * LANES
        return slice(start, start + self.hours)


def head_kernel(lay, left_ref, section_ref, slab_hbm, start_hbm, work, *results):
    messages = results[: lay.parts]
    slab_ref, start_ref, arrived = results[lay.parts :]
    width, hours = lay.width, lay.hours
    copies = [pltpu.make_async_copy(start_hbm, start_ref, arrived.at[lay.parts])]
    for part in range(lay.parts):
        span = lay.part(part)
        copies.append(pltpu.make_async_copy(slab_hbm.at[:, span], slab_ref.at[:, span], arrived.at[part]))
    for copy in copies:
        copy.start()
    left = left_ref[0] != 0
    outgoing, incoming, inverse, keep, swap, diagonal = tables(section_ref, hours)
    later = lax.broadcasted_iota(jnp.int32, (hours, hours), 0)
    earlier = lax.broadcasted_iota(jnp.int32, (hours, hours), 1)
    columns = jnp.transpose(outgoing[:, :hours])
    full = outer(columns, inverse[:, :hours])
    full = jnp.where(later > earlier, full, jnp.where(later == earlier, diagonal, 0.0))
    copies[0].wait()
    start = start_ref[...].astype(jnp.float32)
    weights = jnp.dot(start, full, precision=TOP)
    handed = jnp.transpose(jnp.dot(start, columns, precision=TOP))
    handed = jnp.concatenate([handed, jnp.zeros((STATES, LANES - width), jnp.float32)], axis=1)
    weights = jnp.concatenate([weights, incoming[:, :hours]], axis=0)
    high = weights.astype(jnp.bfloat16)
    low = (weights - high.astype(jnp.float32)).astype(jnp.bfloat16)
    for part in range(lay.parts):
        span = lay.part(part)
        copies[part + 1].wait()
        block = slab_ref[:, span]
        total = jnp.dot(high, block, preferred_element_type=jnp.float32) + jnp.dot(
            low, block, preferred_element_type=jnp.float32
        )
        work[: width + STATES, span] = total
        padded = jnp.concatenate([handed, jnp.zeros((STATES, lay.part_cells - LANES), jnp.float32)], axis=1)
        extra = doubled(jnp.where(left, total[width:], padded))
        messages[part][...] = jnp.concatenate([total[:width], extra], axis=0).astype(jnp.bfloat16)
    work[lay.enter, : lay.cells] = jnp.zeros((STATES, lay.cells), jnp.float32)
    for block in range(lay.blocks):
        work[:width, lay.filter_block(block)] = full[block * width : (block + 1) * width]
    table = work.at[:, lay.table : lay.table + LANES]
    for place, value in enumerate((outgoing, handed, keep, swap)):
        table[place * STATES : (place + 1) * STATES, :] = value


def column_of(rows, width):
    return jnp.transpose(rows[:, :LANES])[:width]


def inward_kernel(lay, part, hop, line, place_ref, recv_ref, _, work, message_ref):
    width, span = lay.width, lay.part(part)
    place = place_ref[0]
    left = place == hop + 1

    @pl.when(left | (place == line - 2 - hop))
    def _():
        received = recv_ref[...].astype(jnp.float32)
        states = joined(received[width:])
        states_own = work[lay.own, span]
        handed = lay.rows(work, 1)
        columns = column_of(jnp.where(left, handed, states[:, :LANES]), width)
        rows = jnp.where(left, states, states_own)
        total = received[:width] + work[:width, span] + outer(columns, rows)
        padded = jnp.concatenate([handed, jnp.zeros((STATES, lay.part_cells - LANES), jnp.float32)], axis=1)
        swap = lay.rows(work, 3)[:, 0:1]
        extra = advanced(states, lay.rows(work, 2)[:, 0:1], jnp.where(left, swap, -swap))
        extra = extra + jnp.where(left, states_own, padded)
        message_ref[...] = jnp.concatenate([total, doubled(extra)], axis=0).astype(jnp.bfloat16)
        work[:width, span] = total
        work[lay.out, span] = extra
        work[lay.enter, span] = jnp.where(left, states, 0.0)


def middle_kernel(lay, part, line, place_ref, recv_ref, _, work, message_ref):
    width, span = lay.width, lay.part(part)
    place = place_ref[0]
    left = place == line // 2 - 1

    @pl.when(left | (place == line // 2))
    def _():
        received = recv_ref[...].astype(jnp.float32)
        states = joined(received[width:])
        handed = work[lay.out, span]
        columns = column_of(jnp.where(left, states[:, :LANES], handed[:, :LANES]), width)
        total = received[:width] + work[:width, span] + outer(columns, jnp.where(left, handed, states))
        extra = advanced(states, lay.rows(work, 2)[:, 0:1], lay.rows(work, 3)[:, 0:1]) + work[lay.own, span]
        message_ref[...] = jnp.concatenate([total, doubled(extra)], axis=0).astype(jnp.bfloat16)
        work[:width, span] = total

        @pl.when(jnp.logical_not(left))
        def _():
            work[lay.enter, span] = states


def outward_kernel(lay, part, hop, line, place_ref, recv_ref, _, work, message_ref):
    width, span = lay.width, lay.part(part)
    place = place_ref[0]
    right = place == line // 2 + 1 + hop

    @pl.when(right | (place == line // 2 - 2 - hop))
    def _():
        received = recv_ref[...].astype(jnp.float32)
        states = joined(received[width:])
        extra = advanced(states, lay.rows(work, 2)[:, 0:1], lay.rows(work, 3)[:, 0:1]) + work[lay.own, span]
        message_ref[...] = jnp.concatenate([received[:width], doubled(extra)], axis=0).astype(jnp.bfloat16)
        work[:width, span] = received[:width]

        @pl.when(right)
        def _():
            work[lay.enter, span] = states


def packed_shape(width, hours):
    return (width + width // 2, hours) if hours == 2 * width else (width, hours + width)


def packed(filtered, gram):
    width, hours = filtered.shape
    if hours == 2 * width:
        halves = jnp.concatenate([gram[: width // 2], gram[width // 2 :]], axis=1)
        return jnp.concatenate([filtered, halves], axis=0)
    return jnp.concatenate([filtered, gram], axis=1)


def unpacked(sums, width, hours):
    if hours == 2 * width:
        halves = sums[width:]
        return sums[:width], jnp.concatenate([halves[:, :width], halves[:, width:]], axis=0)
    return sums[:, :hours], sums[:, hours:]


def gather_kernel(lay, part, line, place_ref, slab_ref, recv_ref, _, work, *results):
    width, hours, span = lay.width, lay.hours, lay.part(part)
    place = place_ref[0]
    last_left, last_right = place == 0, place == line - 1
    outermost = (last_left | last_right) if line > 2 else False
    patterns = jnp.where(outermost, recv_ref[:width], work[:width, span].astype(jnp.bfloat16))
    states = work[lay.enter, span]
    if line > 2:
        states = jnp.where(last_right, joined(recv_ref[...].astype(jnp.float32)[width:]), states)

        @pl.when(outermost & (place == part))
        def _():
            work[:width, span] = patterns.astype(jnp.float32)

    def product(value):
        return lax.dot_general(patterns, value, (((1,), (1,)), ((), ())), preferred_element_type=jnp.float32)

    blocks = (product(slab_ref[...]), product(patterns), product(doubled(states).astype(jnp.bfloat16)))
    sums = jnp.concatenate(blocks, axis=1)
    running = slice(lay.running, lay.running + hours + width + STATES)
    if part:
        sums = work[:width, running] + sums
    if part < lay.parts - 1:
        work[:width, running] = sums
        return
    sums_ref, own_ref = results
    over_states = (((1,), (1,)), ((), ()))
    filtered = [
        lax.dot_general(sums[:, :hours], work[:width, lay.filter_block(block)], over_states, precision=TOP)
        for block in range(lay.blocks)
    ]
    filtered = filtered[0] if lay.blocks == 1 else jnp.concatenate(filtered, axis=1)
    entering = jnp.dot(sums[:, hours + width :], lay.rows(work, 0)[:, :hours], precision=TOP)
    sums_ref[...] = packed(filtered + entering, sums[:, hours : hours + width])
    own_ref[...] = work[:width, pl.ds(pl.multiple_of(place * lay.part_cells, LANES), lay.part_cells)]


def inverse_factor(gram):
    width = gram.shape[0]
    row = lax.broadcasted_iota(jnp.int32, (width, width), 0)
    column = lax.broadcasted_iota(jnp.int32, (width, width), 1)
    work = jnp.concatenate([gram, jnp.where(row == column, 1.0, 0.0)], axis=1)
    index = lax.broadcasted_iota(jnp.int32, (width, 1), 0)
    for k in range(width - 1):
        pivot = work[k : k + 1, :]
        factor = jnp.where(index > k, work[:, k : k + 1] / pivot[:, k : k + 1], 0.0)
        work = work - factor * pivot
    diagonal = jnp.sum(jnp.where(row == column, work[:, :width], 0.0), axis=1, keepdims=True)
    return work[:, width:] * lax.rsqrt(diagonal)


def tail_kernel(basis_scale, pcs_scale, one_ref, two_ref, own_ref, basis_ref, pcs_ref):
    width = own_ref.shape[0]
    sums = one_ref[...] + two_ref[...]
    filtered, gram = unpacked(sums, width, pcs_ref.shape[1])
    inverse = inverse_factor(gram)
    pcs_ref[...] = jnp.dot(inverse * pcs_scale, filtered, precision=TOP)
    basis = jnp.dot(inverse * basis_scale, own_ref[...], precision=TOP)
    for group in range(basis_ref.shape[0]):
        basis_ref[group] = basis[:, group * LANES : (group + 1) * LANES]


def call(kernel, name, out_shape, *args, scalars=1, far=0, scratch=(), in_place=False, final=False):
    smem, vmem = pl.BlockSpec(memory_space=pltpu.SMEM), pl.BlockSpec(memory_space=pltpu.VMEM)
    hbm = pl.BlockSpec(memory_space=pltpu.HBM)
    count = len(args)
    keep = pltpu.with_memory_space_constraint
    args = list(args[:scalars]) + [
        keep(arg, pltpu.HBM if place < far else pltpu.VMEM) for place, arg in enumerate(args[scalars:])
    ]
    return pl.pallas_call(
        kernel,
        out_shape=out_shape if final else [pltpu.VMEM(out.shape, out.dtype) for out in out_shape],
        in_specs=[smem] * scalars + [hbm] * far + [vmem] * (count - scalars - far),
        out_specs=[vmem] * len(out_shape),
        scratch_shapes=scratch,
        input_output_aliases={count - 1: 0} if in_place else {},
        compiler_params=pltpu.CompilerParams(vmem_limit_bytes=VMEM_LIMIT),
        cost_estimate=pl.CostEstimate(flops=1, bytes_accessed=1, transcendentals=0),
        name=name,
    )(*args)


def complete(moves, size, both):
    moves = moves + [(target, source) for source, target in moves] if both else moves
    used = {device for move in moves for device in move}
    return moves + [(device, device) for device in range(size) if device not in used]


def local(slab, start, sections):
    hours, cells = slab.shape
    width = start.shape[1]
    line = lax.axis_size("tm")
    half = line // 2
    parts = line
    lay = Layout(hours, cells, width, parts)
    f32, bf16 = jnp.float32, jnp.bfloat16
    shape = jax.ShapeDtypeStruct
    place = lax.axis_index("tm").astype(jnp.int32).reshape(1)
    left = (place < half).astype(jnp.int32)
    work_shape, message_shape = shape(lay.shape, f32), shape((width + STATES, lay.part_cells), bf16)

    work, *messages = call(
        functools.partial(head_kernel, lay), "head", [work_shape] + [message_shape] * parts,
        left, sections.T, slab, start.T, scalars=2, far=2,
        scratch=[pltpu.VMEM(slab.shape, bf16), pltpu.VMEM((width, hours), bf16), pltpu.SemaphoreType.DMA((parts + 1,))],
    )
    results = [work_shape, message_shape]

    def send(message, moves, both):
        return lax.ppermute(message, "tm", complete(moves, line, both))

    def inward_moves(hop):
        return [(hop, hop + 1), (line - 1 - hop, line - 2 - hop)]

    def inward(part, work):
        block = arriving[part]
        for hop in range(half - 1):
            kernel = functools.partial(inward_kernel, lay, part, hop, line)
            work, message = call(kernel, "inward", results, place, block, work, in_place=True)
            if hop < half - 2:
                block = send(message, inward_moves(hop + 1), True)
        arriving[part] = send(message if half > 1 else messages[part], [(half - 1, half), (half, half - 1)], False)
        return work

    def middle(part, work):
        kernel = functools.partial(middle_kernel, lay, part, line)
        work, message = call(kernel, "middle", results, place, arriving[part], work, in_place=True)
        for hop in range(half - 1):
            moves = [(half - 1 - hop, half - 2 - hop), (half + hop, half + 1 + hop)]
            arriving[part] = send(message, moves, part > 0)
            if hop < half - 2:
                kernel = functools.partial(outward_kernel, lay, part, hop, line)
                work, message = call(kernel, "outward", results, place, arriving[part], work, in_place=True)
        return work

    def gather(part, work):
        shapes = [work_shape]
        if part == parts - 1:
            shapes += [shape(packed_shape(width, hours), f32), shape((width, lay.part_cells), f32)]
        kernel = functools.partial(gather_kernel, lay, part, line)
        return call(kernel, "gather", shapes, place, slab[:, lay.part(part)], arriving[part], work, in_place=True)

    arriving = [send(message, inward_moves(0), True) if half > 1 else message for message in messages]
    for step in range(parts + 1):
        if step < parts:
            work = inward(step, work)
        if step:
            work = middle(step - 1, work)
        if step == parts - 1:
            (work,) = gather(0, work)
    for part in range(1, parts):
        work, *rest = gather(part, work)
    running, own = rest

    steps = []
    for axis in ("lon", "lat"):
        size, stride = lax.axis_size(axis), 1
        while stride < size:
            steps.append((axis, [(i, i ^ stride) for i in range(size)]))
            stride *= 2
    for axis, moves in steps[:-1]:
        running = running + lax.ppermute(running, axis, moves)
    other = lax.ppermute(running, *steps[-1])

    part_cells = lay.part_cells
    cells_all = cells * lax.axis_size("lat") * lax.axis_size("lon")
    basis, pcs = call(
        functools.partial(tail_kernel, math.sqrt(cells_all), math.sqrt(hours * line / cells_all)), "tail",
        [shape((part_cells // LANES, width, LANES), f32), shape((width, hours), f32)],
        running, other, own, scalars=0, final=True,
    )
    return (basis, pcs.T)


def solution(mesh):
    return jax.shard_map(
        local,
        mesh=mesh,
        in_specs=(P("tm", ("lat", "lon")), P("tm", None), P()),
        out_specs=(P(("lat", "lon", "tm"), None, None), P("tm", None)),
        check_vma=False,
    )
```

```python
import functools
import math

import jax
import jax.numpy as jnp
from jax import lax
from jax.experimental import pallas as pl
from jax.experimental.pallas import tpu as pltpu
from jax.sharding import PartitionSpec as P

LANES = 128
STATES = 8
TOP = lax.Precision.HIGHEST
VMEM_LIMIT = 8 * 1024 * 1024
PARTS = 5
LAG = 3


def row_pairs(first, second):
    row = lax.broadcasted_iota(jnp.int32, (STATES, LANES), 0)
    return jnp.where(row % 4 < 2, first, second)


def swapped(value):
    row = lax.broadcasted_iota(jnp.int32, value.shape, 0)
    return jnp.where(row % 2 == 0, pltpu.roll(value, STATES - 1, 0), pltpu.roll(value, 1, 0))


def tables(section_ref, hours):
    shape = (STATES, LANES)
    radius, angle, amplitude = (row_pairs(section_ref[0, i], section_ref[1, i]) for i in range(3))
    hour = lax.broadcasted_iota(jnp.int32, shape, 1).astype(jnp.float32)
    imaginary = lax.broadcasted_iota(jnp.int32, shape, 0) % 2 == 1
    sign = jnp.where(imaginary, 1.0, -1.0)
    drive = amplitude * jnp.sqrt(1.0 - radius * radius)
    back = 1.0 / (radius * radius)
    gain_re = drive * (1.0 + back)
    gain_im = -drive * (1.0 - back) * jnp.cos(angle) / jnp.sin(angle)
    log_radius = jnp.log(radius)

    def power(n):
        turn = n * angle
        return jnp.exp(n * log_radius) * jnp.where(imaginary, jnp.sin(turn), jnp.cos(turn))

    ahead = power(hour)
    outgoing = -sign * (gain_re * ahead + sign * gain_im * swapped(ahead))
    inverse, incoming = power(-hour), power(hours - hour)
    lam = power(jnp.full(shape, hours, jnp.float32))
    keep = jnp.where(imaginary, swapped(lam), lam)
    swap = sign * jnp.where(imaginary, lam, swapped(lam))
    diagonal = drive[0:1, 0:1] + drive[2:3, 0:1]
    return outgoing, incoming, inverse, keep, swap, diagonal


def doubled(value):
    rounded = value.astype(jnp.bfloat16).astype(jnp.float32)
    row = lax.broadcasted_iota(jnp.int32, value.shape, 0)
    return jnp.where(row < STATES // 2, rounded, value - rounded)


def joined(value):
    return value + pltpu.roll(value, STATES // 2, 0)


def advanced(value, keep, swap):
    return keep * value + swap * swapped(value)


def outer(columns, rows):
    total = columns[:, 0:1] * rows[0:1, :]
    for k in range(1, STATES // 2):
        total = total + columns[:, k : k + 1] * rows[k : k + 1, :]
    return total


class Layout:
    def __init__(self, hours, cells, width, parts, line):
        self.hours, self.width, self.parts, self.cells = hours, width, parts, cells
        self.size = -(-cells // (parts * LANES)) * LANES
        self.own_cells = cells // line
        self.own = slice(width, width + STATES)
        self.out = slice(width + STATES, width + 2 * STATES)
        self.enter = slice(width + 2 * STATES, width + 3 * STATES)
        self.blocks = hours // width
        self.filter = parts * self.size
        self.table = self.filter + self.blocks * LANES
        self.weights = self.table + LANES
        self.running = self.weights + LANES
        self.columns = self.running + LANES * (-(-(hours + width + STATES) // LANES))
        self.shape = (width + 3 * STATES, self.columns)

    def part(self, part):
        return slice(part * self.size, (part + 1) * self.size)

    def real(self, part):
        return slice(part * self.size, min((part + 1) * self.size, self.cells))

    def rows(self, work, place):
        return work[place * STATES : (place + 1) * STATES, self.table : self.table + LANES]

    def filter_block(self, block):
        start = self.filter + block * LANES
        return slice(start, start + self.hours)


def add_part(lay, part, left, slab_ref, work, message_ref):
    width, span, real = lay.width, lay.part(part), lay.real(part)
    weights = work[: width + STATES, lay.weights : lay.weights + lay.hours]
    high = weights.astype(jnp.bfloat16)
    low = (weights - high.astype(jnp.float32)).astype(jnp.bfloat16)
    block = slab_ref[:, real]
    total = jnp.dot(high, block, preferred_element_type=jnp.float32) + jnp.dot(
        low, block, preferred_element_type=jnp.float32
    )
    if real != span:
        past = jnp.zeros((width + STATES, span.stop - real.stop), jnp.float32)
        total = jnp.concatenate([total, past], axis=1)
    work[: width + STATES, span] = total
    padded = jnp.concatenate([lay.rows(work, 1), jnp.zeros((STATES, lay.size - LANES), jnp.float32)], axis=1)
    extra = doubled(jnp.where(left, total[width:], padded))
    message_ref[...] = jnp.concatenate([total[:width], extra], axis=0).astype(jnp.bfloat16)


def head_kernel(lay, left_ref, section_hbm, slab_hbm, start_hbm, work, message_ref, *scratch):
    slab_ref, start_ref, section_ref, arrived = scratch
    width, hours = lay.width, lay.hours
    copies = [
        pltpu.make_async_copy(section_hbm, section_ref, arrived.at[0]),
        pltpu.make_async_copy(start_hbm, start_ref, arrived.at[1]),
        pltpu.make_async_copy(slab_hbm.at[:, lay.part(0)], slab_ref, arrived.at[2]),
    ]
    for copy in copies:
        copy.start()
    left = left_ref[0] != 0
    work[lay.enter, : lay.filter] = jnp.zeros((STATES, lay.filter), jnp.float32)
    copies[0].wait()
    outgoing, incoming, inverse, keep, swap, diagonal = tables(section_ref, hours)
    later = lax.broadcasted_iota(jnp.int32, (hours, hours), 0)
    earlier = lax.broadcasted_iota(jnp.int32, (hours, hours), 1)
    columns = jnp.transpose(outgoing[:, :hours])
    full = outer(columns, inverse[:, :hours])
    full = jnp.where(later > earlier, full, jnp.where(later == earlier, diagonal, 0.0))
    copies[1].wait()
    start = start_ref[...].astype(jnp.float32)
    work[:width, lay.weights : lay.weights + hours] = jnp.dot(start, full, precision=TOP)
    work[width : width + STATES, lay.weights : lay.weights + hours] = incoming[:, :hours]
    handed = jnp.transpose(jnp.dot(start, columns, precision=TOP))
    handed = jnp.concatenate([handed, jnp.zeros((STATES, LANES - width), jnp.float32)], axis=1)
    for block in range(lay.blocks):
        work[:width, lay.filter_block(block)] = full[block * width : (block + 1) * width]
    table = work.at[:, lay.table : lay.table + LANES]
    for place, value in enumerate((outgoing, handed, keep, swap)):
        table[place * STATES : (place + 1) * STATES, :] = value
    copies[2].wait()
    add_part(lay, 0, left, slab_ref, work, message_ref)


def rest_kernel(lay, left_ref, slab_hbm, _, work, *refs):
    messages, (slab_ref, arrived) = refs[: lay.parts - 1], refs[lay.parts - 1 :]
    copies = []
    for part in range(1, lay.parts):
        real = lay.real(part)
        copies.append(pltpu.make_async_copy(slab_hbm.at[:, real], slab_ref.at[:, real], arrived.at[part - 1]))
        copies[-1].start()
    for part in range(1, lay.parts):
        copies[part - 1].wait()
        add_part(lay, part, left_ref[0] != 0, slab_ref, work, messages[part - 1])


def column_of(rows, width):
    return jnp.transpose(rows[:, :LANES])[:width]


def inward_kernel(lay, part, hop, line, place_ref, recv_ref, _, work, message_ref):
    width, span = lay.width, lay.part(part)
    place = place_ref[0]
    left = place == hop + 1

    @pl.when(left | (place == line - 2 - hop))
    def _():
        received = recv_ref[...].astype(jnp.float32)
        states = joined(received[width:])
        states_own = work[lay.own, span]
        handed = lay.rows(work, 1)
        columns = column_of(jnp.where(left, handed, states[:, :LANES]), width)
        rows = jnp.where(left, states, states_own)
        total = received[:width] + work[:width, span] + outer(columns, rows)
        padded = jnp.concatenate([handed, jnp.zeros((STATES, lay.size - LANES), jnp.float32)], axis=1)
        swap = lay.rows(work, 3)[:, 0:1]
        extra = advanced(states, lay.rows(work, 2)[:, 0:1], jnp.where(left, swap, -swap))
        extra = extra + jnp.where(left, states_own, padded)
        message_ref[...] = jnp.concatenate([total, doubled(extra)], axis=0).astype(jnp.bfloat16)
        work[:width, span] = total
        work[lay.out, span] = extra
        work[lay.enter, span] = jnp.where(left, states, 0.0)


def middle_kernel(lay, part, line, place_ref, recv_ref, *refs):
    work, message_ref = refs[-2:]
    width, span = lay.width, lay.part(part)
    place = place_ref[0]
    left = place == line // 2 - 1

    @pl.when(left | (place == line // 2))
    def _():
        received = recv_ref[...].astype(jnp.float32)
        states = joined(received[width:])
        handed = work[lay.out, span]
        columns = column_of(jnp.where(left, states[:, :LANES], handed[:, :LANES]), width)
        total = received[:width] + work[:width, span] + outer(columns, jnp.where(left, handed, states))
        extra = advanced(states, lay.rows(work, 2)[:, 0:1], lay.rows(work, 3)[:, 0:1]) + work[lay.own, span]
        message_ref[...] = jnp.concatenate([total, doubled(extra)], axis=0).astype(jnp.bfloat16)
        work[:width, span] = total

        @pl.when(jnp.logical_not(left))
        def _():
            work[lay.enter, span] = states


def outward_kernel(lay, part, hop, line, place_ref, recv_ref, _, work, message_ref):
    width, span = lay.width, lay.part(part)
    place = place_ref[0]
    right = place == line // 2 + 1 + hop

    @pl.when(right | (place == line // 2 - 2 - hop))
    def _():
        received = recv_ref[...].astype(jnp.float32)
        states = joined(received[width:])
        extra = advanced(states, lay.rows(work, 2)[:, 0:1], lay.rows(work, 3)[:, 0:1]) + work[lay.own, span]
        message_ref[...] = jnp.concatenate([received[:width], doubled(extra)], axis=0).astype(jnp.bfloat16)
        work[:width, span] = received[:width]

        @pl.when(right)
        def _():
            work[lay.enter, span] = states


def packed_shape(width, hours):
    return (width + width // 2, hours) if hours == 2 * width else (width, hours + width)


def packed(filtered, gram):
    width, hours = filtered.shape
    if hours == 2 * width:
        halves = jnp.concatenate([gram[: width // 2], gram[width // 2 :]], axis=1)
        return jnp.concatenate([filtered, halves], axis=0)
    return jnp.concatenate([filtered, gram], axis=1)


def unpacked(sums, width, hours):
    if hours == 2 * width:
        halves = sums[width:]
        return sums[:width], jnp.concatenate([halves[:, :width], halves[:, width:]], axis=0)
    return sums[:, :hours], sums[:, hours:]


def gather_kernel(lay, part, line, place_ref, slab_ref, recv_ref, _, work, *results):
    width, hours, span = lay.width, lay.hours, lay.part(part)
    place = place_ref[0]
    last_left, last_right = place == 0, place == line - 1
    outermost = (last_left | last_right) if line > 2 else False
    patterns = jnp.where(outermost, recv_ref[:width], work[:width, span].astype(jnp.bfloat16))
    states = work[lay.enter, span]
    if line > 2:
        states = jnp.where(last_right, joined(recv_ref[...].astype(jnp.float32)[width:]), states)

        @pl.when(outermost)
        def _():
            work[:width, span] = patterns.astype(jnp.float32)

    def product(value):
        return lax.dot_general(patterns, value, (((1,), (1,)), ((), ())), preferred_element_type=jnp.float32)

    cells = slab_ref.shape[1]
    slab_sums = lax.dot_general(
        patterns[:, :cells], slab_ref[...], (((1,), (1,)), ((), ())), preferred_element_type=jnp.float32
    )
    blocks = (slab_sums, product(patterns), product(doubled(states).astype(jnp.bfloat16)))
    sums = jnp.concatenate(blocks, axis=1)
    running = slice(lay.running, lay.running + hours + width + STATES)
    if part:
        sums = work[:width, running] + sums
    if part < lay.parts - 1:
        work[:width, running] = sums
        return
    sums_ref, own_ref = results
    over_states = (((1,), (1,)), ((), ()))
    filtered = [
        lax.dot_general(sums[:, :hours], work[:width, lay.filter_block(block)], over_states, precision=TOP)
        for block in range(lay.blocks)
    ]
    filtered = filtered[0] if lay.blocks == 1 else jnp.concatenate(filtered, axis=1)
    entering = jnp.dot(sums[:, hours + width :], lay.rows(work, 0)[:, :hours], precision=TOP)
    sums_ref[...] = packed(filtered + entering, sums[:, hours : hours + width])
    own_ref[...] = work[:width, pl.ds(pl.multiple_of(place * lay.own_cells, LANES), lay.own_cells)]


def inverse_factor(gram):
    width = gram.shape[0]
    row = lax.broadcasted_iota(jnp.int32, (width, width), 0)
    column = lax.broadcasted_iota(jnp.int32, (width, width), 1)
    work = jnp.concatenate([gram, jnp.where(row == column, 1.0, 0.0)], axis=1)
    tiles = [work[place : place + STATES] for place in range(0, width, STATES)]
    done = []
    for first in range(0, width, STATES):
        block = first // STATES
        spread = [
            [jnp.broadcast_to(tile[:, first + q : first + q + 1], tile.shape) for q in range(STATES)]
            for tile in tiles[block:]
        ]
        rows = [tiles[block][q : q + 1] for q in range(STATES)]
        value = [[spread[0][q][p : p + 1] for q in range(p + 1)] for p in range(STATES)]
        over, low = [None] * STATES, [[None] * STATES for _ in range(STATES)]
        for p in range(STATES):
            over[p] = 1.0 / value[p][p]
            done.append(rows[p] * lax.rsqrt(value[p][p]))
            for q in range(p + 1, STATES):
                low[q][p] = value[q][p] * over[p]
                rows[q] = rows[q] - low[q][p] * rows[p]
                for t in range(p + 1, q + 1):
                    value[q][t] = value[q][t] - low[q][p] * value[t][p]
        solved = [rows[p] * over[p] for p in range(STATES)]
        for p in reversed(range(STATES)):
            for q in range(p + 1, STATES):
                solved[p] = solved[p] - low[q][p] * solved[q]
        for place in range(block + 1, len(tiles)):
            for q in range(STATES):
                tiles[place] = tiles[place] - spread[place - block][q] * solved[q]
    return jnp.concatenate(done, axis=0)[:, width:]


def tail_kernel(basis_scale, pcs_scale, one_ref, two_ref, own_ref, basis_ref, pcs_ref):
    width = own_ref.shape[0]
    sums = one_ref[...] + two_ref[...]
    filtered, gram = unpacked(sums, width, pcs_ref.shape[1])
    inverse = inverse_factor(gram)
    pcs_ref[...] = jnp.dot(inverse * pcs_scale, filtered, precision=TOP)
    basis = jnp.dot(inverse * basis_scale, own_ref[...], precision=TOP)
    for group in range(basis_ref.shape[0]):
        basis_ref[group] = basis[:, group * LANES : (group + 1) * LANES]


def call(kernel, name, out_shape, *args, scalars=1, far=0, scratch=(), in_place=0, final=False):
    smem, vmem = pl.BlockSpec(memory_space=pltpu.SMEM), pl.BlockSpec(memory_space=pltpu.VMEM)
    hbm = pl.BlockSpec(memory_space=pltpu.HBM)
    count = len(args)
    keep = pltpu.with_memory_space_constraint
    args = list(args[:scalars]) + [
        keep(arg, pltpu.HBM if place < far else pltpu.VMEM) for place, arg in enumerate(args[scalars:])
    ]
    return pl.pallas_call(
        kernel,
        out_shape=out_shape if final else [pltpu.VMEM(out.shape, out.dtype) for out in out_shape],
        in_specs=[smem] * scalars + [hbm] * far + [vmem] * (count - scalars - far),
        out_specs=[vmem] * len(out_shape),
        scratch_shapes=scratch,
        input_output_aliases={count - in_place + place: place for place in range(in_place)},
        compiler_params=pltpu.CompilerParams(vmem_limit_bytes=VMEM_LIMIT),
        cost_estimate=pl.CostEstimate(flops=1, bytes_accessed=1, transcendentals=0),
        name=name,
    )(*args)


def complete(moves, size, cores, both):
    moves = moves + [(target, source) for source, target in moves] if both else moves
    used = {device for move in moves for device in move}
    full = [(source * cores + core, target * cores + core) for source, target in moves for core in range(cores)]
    other = 1 if cores % 2 == 0 else 0
    idle = [device * cores + core for device in range(size) if device not in used for core in range(cores)]
    return full + [(device, device ^ other) for device in idle]


def local(slab, start, sections):
    hours, cells = slab.shape
    width = start.shape[1]
    line = lax.axis_size("tm")
    half = line // 2
    parts = PARTS
    lay = Layout(hours, cells, width, parts, line)
    f32, bf16 = jnp.float32, jnp.bfloat16
    shape = jax.ShapeDtypeStruct
    place = lax.axis_index("tm").astype(jnp.int32).reshape(1)
    left = (place < half).astype(jnp.int32)
    work_shape = shape(lay.shape, f32)
    message_shape = shape((width + STATES, lay.size), bf16)
    work, message = call(
        functools.partial(head_kernel, lay), "head", [work_shape, message_shape], left, sections.T, slab, start.T, far=3,
        scratch=[
            pltpu.VMEM((hours, lay.size), bf16), pltpu.VMEM((width, hours), bf16), pltpu.SMEM((2, 3), f32),
            pltpu.SemaphoreType.DMA((3,)),
        ],
    )
    work, *messages = call(
        functools.partial(rest_kernel, lay), "rest", [work_shape] + [message_shape] * (parts - 1), left, slab, work, far=1,
        in_place=1, scratch=[pltpu.VMEM(slab.shape, bf16), pltpu.SemaphoreType.DMA((parts - 1,))],
    )
    messages = [message, *messages]
    results = [work_shape, message_shape]

    def inward_moves(hop):
        return [(hop, hop + 1), (line - 1 - hop, line - 2 - hop)]

    def send(message, moves, both=False):
        return lax.ppermute(message, ("tm", "lon"), complete(moves, line, lax.axis_size("lon"), both))

    def gather(part, block, work):
        shapes = [work_shape]
        if part == parts - 1:
            shapes += [shape(packed_shape(width, hours), f32), shape((width, lay.own_cells), f32)]
        kernel = functools.partial(gather_kernel, lay, part, line)
        return call(kernel, "gather", shapes, place, slab[:, lay.real(part)], block, work, in_place=1)

    def inward(part, hop, block, work):
        kernel = functools.partial(inward_kernel, lay, part, hop, line)
        return call(kernel, "inward", results, place, block, work, in_place=1)

    def middle(part, block, work, *message):
        kernel = functools.partial(middle_kernel, lay, part, line)
        return call(kernel, "middle", results, place, block, work, *message, in_place=1 + len(message))

    middle_moves = [(half - 1, half), (half, half - 1)]
    if half == 2:
        crossing = [send(message, inward_moves(0), True) for message in messages[:LAG]]
        between = [None] * parts
        for step in range(parts + LAG):
            if step < parts:
                work, message = inward(step, 0, crossing[step], work)
                between[step] = send(message, middle_moves)
            if step >= LAG:
                work, *rest = gather(step - LAG, crossing[step], work)
            if 1 <= step <= parts:
                later = step - 1 + LAG
                swapped_in = [messages[later]] if later < parts else []
                work, message = middle(step - 1, between[step - 1], work, *swapped_in)
                crossing.append(send(message, inward_moves(0), True))
    else:
        arriving = [send(message, inward_moves(0)) if half > 1 else message for message in messages]
        for part in range(parts):
            message, block = messages[part], arriving[part]
            for hop in range(half - 1):
                work, message = inward(part, hop, block, work)
                if hop < half - 2:
                    block = send(message, inward_moves(hop + 1))
            block = send(message, middle_moves)
            work, message = middle(part, block, work)
            for hop in range(half - 1):
                block = send(message, [(target, source) for source, target in inward_moves(half - 2 - hop)])
                if hop < half - 2:
                    kernel = functools.partial(outward_kernel, lay, part, hop, line)
                    work, message = call(kernel, "outward", results, place, block, work, in_place=1)
            work, *rest = gather(part, block, work)
    running, own = rest

    steps = []
    for axis in ("lon", "lat"):
        size, stride = lax.axis_size(axis), 1
        while stride < size:
            steps.append((axis, [(i, i ^ stride) for i in range(size)]))
            stride *= 2
    for axis, moves in steps[:-1]:
        running = running + lax.ppermute(running, axis, moves)
    other = lax.ppermute(running, *steps[-1])

    part_cells = lay.own_cells
    cells_all = cells * lax.axis_size("lat") * lax.axis_size("lon")
    basis, pcs = call(
        functools.partial(tail_kernel, math.sqrt(cells_all), math.sqrt(hours * line / cells_all)), "tail",
        [shape((part_cells // LANES, width, LANES), f32), shape((width, hours), f32)],
        running, other, own, scalars=0, final=True,
    )
    return (basis, pcs.T)


def solution(mesh):
    return jax.shard_map(
        local,
        mesh=mesh,
        in_specs=(P("tm", ("lat", "lon")), P("tm", None), P()),
        out_specs=(P(("lat", "lon", "tm"), None, None), P("tm", None)),
        check_vma=False,
    )
```

```python
import functools
import math

import jax
import jax.numpy as jnp
from jax import lax
from jax.experimental import pallas as pl
from jax.experimental.pallas import tpu as pltpu
from jax.sharding import PartitionSpec as P

LANES = 128
STATES = 8
TOP = lax.Precision.HIGHEST
VMEM_LIMIT = 8 * 1024 * 1024
PARTS = 5
LAG = 3


def row_pairs(first, second):
    row = lax.broadcasted_iota(jnp.int32, (STATES, LANES), 0)
    return jnp.where(row % 4 < 2, first, second)


def swapped(value):
    row = lax.broadcasted_iota(jnp.int32, value.shape, 0)
    return jnp.where(row % 2 == 0, pltpu.roll(value, STATES - 1, 0), pltpu.roll(value, 1, 0))


def tables(section_ref, hours):
    shape = (STATES, LANES)
    radius, angle, amplitude = (row_pairs(section_ref[0, i], section_ref[1, i]) for i in range(3))
    hour = lax.broadcasted_iota(jnp.int32, shape, 1).astype(jnp.float32)
    imaginary = lax.broadcasted_iota(jnp.int32, shape, 0) % 2 == 1
    sign = jnp.where(imaginary, 1.0, -1.0)
    drive = amplitude * jnp.sqrt(1.0 - radius * radius)
    back = 1.0 / (radius * radius)
    gain_re = drive * (1.0 + back)
    gain_im = -drive * (1.0 - back) * jnp.cos(angle) / jnp.sin(angle)
    log_radius = jnp.log(radius)

    def power(n):
        turn = n * angle
        return jnp.exp(n * log_radius) * jnp.where(imaginary, jnp.sin(turn), jnp.cos(turn))

    ahead = power(hour)
    outgoing = -sign * (gain_re * ahead + sign * gain_im * swapped(ahead))
    inverse, incoming = power(-hour), power(hours - hour)
    lam = power(jnp.full(shape, hours, jnp.float32))
    keep = jnp.where(imaginary, swapped(lam), lam)
    swap = sign * jnp.where(imaginary, lam, swapped(lam))
    diagonal = drive[0:1, 0:1] + drive[2:3, 0:1]
    return outgoing, incoming, inverse, keep, swap, diagonal


def doubled(value):
    rounded = value.astype(jnp.bfloat16).astype(jnp.float32)
    row = lax.broadcasted_iota(jnp.int32, value.shape, 0)
    return jnp.where(row < STATES // 2, rounded, value - rounded)


def joined(value):
    return value + pltpu.roll(value, STATES // 2, 0)


def extra_columns(cells, width):
    tiles = -(-cells // (2 * LANES))
    return -(-tiles // (width // STATES)) * LANES


def packed_rows(rows, width):
    cells = rows.shape[1]
    upper = lax.broadcasted_iota(jnp.int32, (STATES, LANES), 0) < STATES // 2
    zero = jnp.zeros((STATES, LANES), jnp.float32)
    groups = [rows[:, start : start + LANES] for start in range(0, cells, LANES)] + [zero]
    tiles = [jnp.where(upper, groups[i], groups[i + 1]) for i in range(0, len(groups) - 1, 2)]
    tall = width // STATES
    columns = extra_columns(cells, width) // LANES
    tiles += [zero] * (tall * columns - len(tiles))
    blocks = [jnp.concatenate(tiles[i * tall : (i + 1) * tall], axis=0) for i in range(columns)]
    return blocks[0] if columns == 1 else jnp.concatenate(blocks, axis=1)


def spread_rows(block, cells):
    upper = lax.broadcasted_iota(jnp.int32, (STATES, LANES), 0) < STATES // 2
    tall = block.shape[0] // STATES
    groups = []
    for group in range(cells // LANES):
        column, tile = divmod(group // 2, tall)
        value = block[tile * STATES : (tile + 1) * STATES, column * LANES : (column + 1) * LANES]
        groups.append(joined(jnp.where(upper if group % 2 == 0 else jnp.logical_not(upper), value, 0.0)))
    return jnp.concatenate(groups, axis=1)


def advanced(value, keep, swap):
    return keep * value + swap * swapped(value)


def outer(columns, rows):
    total = columns[:, 0:1] * rows[0:1, :]
    for k in range(1, STATES // 2):
        total = total + columns[:, k : k + 1] * rows[k : k + 1, :]
    return total


class Layout:
    def __init__(self, hours, cells, width, parts, line):
        self.hours, self.width, self.parts, self.cells = hours, width, parts, cells
        self.size = -(-cells // (parts * LANES)) * LANES
        self.own_cells = cells // line
        self.own = slice(width, width + STATES)
        self.out = slice(width + STATES, width + 2 * STATES)
        self.enter = slice(width + 2 * STATES, width + 3 * STATES)
        self.blocks = hours // width
        self.filter = parts * self.size
        self.table = self.filter + self.blocks * LANES
        self.weights = self.table + LANES
        self.running = self.weights + LANES
        self.columns = self.running + LANES * (-(-(hours + width + STATES) // LANES))
        self.shape = (width + 3 * STATES, self.columns)

    def part(self, part):
        return slice(part * self.size, (part + 1) * self.size)

    def real(self, part):
        return slice(part * self.size, min((part + 1) * self.size, self.cells))

    def rows(self, work, place):
        return work[place * STATES : (place + 1) * STATES, self.table : self.table + LANES]

    def filter_block(self, block):
        start = self.filter + block * LANES
        return slice(start, start + self.hours)


def add_part(lay, part, left, slab_ref, work, message_ref):
    width, span, real = lay.width, lay.part(part), lay.real(part)
    weights = work[: width + STATES, lay.weights : lay.weights + lay.hours]
    high = weights.astype(jnp.bfloat16)
    low = (weights - high.astype(jnp.float32)).astype(jnp.bfloat16)
    block = slab_ref[:, real]
    total = jnp.dot(high, block, preferred_element_type=jnp.float32) + jnp.dot(
        low, block, preferred_element_type=jnp.float32
    )
    if real != span:
        past = jnp.zeros((width + STATES, span.stop - real.stop), jnp.float32)
        total = jnp.concatenate([total, past], axis=1)
    work[: width + STATES, span] = total
    padded = jnp.concatenate([lay.rows(work, 1), jnp.zeros((STATES, lay.size - LANES), jnp.float32)], axis=1)
    if message_ref is not None:
        extra = packed_rows(jnp.where(left, total[width:], padded), width)
        message_ref[...] = jnp.concatenate([total[:width], extra], axis=1).astype(jnp.bfloat16)


def begin(lay, left, section_hbm, slab_hbm, start_hbm, work, message_ref, slab_ref, start_ref, section_ref, arrived):
    width, hours = lay.width, lay.hours
    copies = [
        pltpu.make_async_copy(section_hbm, section_ref, arrived.at[0]),
        pltpu.make_async_copy(start_hbm, start_ref, arrived.at[1]),
        pltpu.make_async_copy(slab_hbm.at[:, lay.part(0)], slab_ref.at[:, lay.part(0)], arrived.at[2]),
    ]
    for copy in copies:
        copy.start()
    copies[0].wait()
    outgoing, incoming, inverse, keep, swap, diagonal = tables(section_ref, hours)
    later = lax.broadcasted_iota(jnp.int32, (hours, hours), 0)
    earlier = lax.broadcasted_iota(jnp.int32, (hours, hours), 1)
    columns = jnp.transpose(outgoing[:, :hours])
    full = outer(columns, inverse[:, :hours])
    full = jnp.where(later > earlier, full, jnp.where(later == earlier, diagonal, 0.0))
    copies[1].wait()
    start = start_ref[...].astype(jnp.float32)
    work[:width, lay.weights : lay.weights + hours] = jnp.dot(start, full, precision=TOP)
    work[width : width + STATES, lay.weights : lay.weights + hours] = incoming[:, :hours]
    handed = jnp.transpose(jnp.dot(start, columns, precision=TOP))
    handed = jnp.concatenate([handed, jnp.zeros((STATES, LANES - width), jnp.float32)], axis=1)
    for block in range(lay.blocks):
        work[:width, lay.filter_block(block)] = full[block * width : (block + 1) * width]
    table = work.at[:, lay.table : lay.table + LANES]
    for place, value in enumerate((outgoing, handed, keep, swap)):
        table[place * STATES : (place + 1) * STATES, :] = value
    copies[2].wait()
    add_part(lay, 0, left, slab_ref, work, message_ref)


def head_kernel(lay, line, place_ref, section_hbm, slab_hbm, start_hbm, work, message_ref, *scratch):
    place = place_ref[0]

    @pl.when((place == 0) | (place == line - 1))
    def _():
        begin(lay, place < line // 2, section_hbm, slab_hbm, start_hbm, work, message_ref, *scratch)


def rest_kernel(lay, line, place_ref, section_hbm, slab_hbm, start_hbm, _, work, *refs):
    messages, scratch = refs[: lay.parts - 1], refs[lay.parts - 1 :]
    slab_ref, landed = scratch[0], scratch[-1]
    place = place_ref[0]
    left = place < line // 2
    copies = []
    for part in range(1, lay.parts):
        real = lay.real(part)
        copies.append(pltpu.make_async_copy(slab_hbm.at[:, real], slab_ref.at[:, real], landed.at[part - 1]))
        copies[-1].start()
    work[lay.enter, : lay.filter] = jnp.zeros((STATES, lay.filter), jnp.float32)

    @pl.when((place != 0) & (place != line - 1))
    def _():
        begin(lay, left, section_hbm, slab_hbm, start_hbm, work, None, *scratch[:-1])

    for part in range(1, lay.parts):
        copies[part - 1].wait()
        add_part(lay, part, left, slab_ref, work, messages[part - 1])


def column_of(rows, width):
    return jnp.transpose(rows[:, :LANES])[:width]


def inward_kernel(lay, part, hop, line, place_ref, recv_ref, _, work, message_ref):
    width, span = lay.width, lay.part(part)
    place = place_ref[0]
    left = place == hop + 1

    @pl.when(left | (place == line - 2 - hop))
    def _():
        received = recv_ref[...].astype(jnp.float32)
        states = spread_rows(received[:, lay.size :], lay.size)
        states_own = work[lay.own, span]
        handed = lay.rows(work, 1)
        columns = column_of(jnp.where(left, handed, states[:, :LANES]), width)
        rows = jnp.where(left, states, states_own)
        total = received[:, : lay.size] + work[:width, span] + outer(columns, rows)
        padded = jnp.concatenate([handed, jnp.zeros((STATES, lay.size - LANES), jnp.float32)], axis=1)
        swap = lay.rows(work, 3)[:, 0:1]
        extra = advanced(states, lay.rows(work, 2)[:, 0:1], jnp.where(left, swap, -swap))
        extra = extra + jnp.where(left, states_own, padded)
        message_ref[...] = jnp.concatenate([total, packed_rows(extra, width)], axis=1).astype(jnp.bfloat16)
        work[:width, span] = total
        work[lay.out, span] = extra
        work[lay.enter, span] = jnp.where(left, states, 0.0)


def middle_kernel(lay, part, line, place_ref, recv_ref, *refs):
    work, message_ref = refs[-2:]
    width, span = lay.width, lay.part(part)
    place = place_ref[0]
    left = place == line // 2 - 1

    @pl.when(left | (place == line // 2))
    def _():
        received = recv_ref[...].astype(jnp.float32)
        states = spread_rows(received[:, lay.size :], lay.size)
        handed = work[lay.out, span]
        columns = column_of(jnp.where(left, states[:, :LANES], handed[:, :LANES]), width)
        total = received[:, : lay.size] + work[:width, span] + outer(columns, jnp.where(left, handed, states))
        extra = advanced(states, lay.rows(work, 2)[:, 0:1], lay.rows(work, 3)[:, 0:1]) + work[lay.own, span]
        message_ref[...] = jnp.concatenate([total, packed_rows(extra, width)], axis=1).astype(jnp.bfloat16)
        work[:width, span] = total

        @pl.when(jnp.logical_not(left))
        def _():
            work[lay.enter, span] = states


def outward_kernel(lay, part, hop, line, place_ref, recv_ref, _, work, message_ref):
    width, span = lay.width, lay.part(part)
    place = place_ref[0]
    right = place == line // 2 + 1 + hop

    @pl.when(right | (place == line // 2 - 2 - hop))
    def _():
        received = recv_ref[...].astype(jnp.float32)
        states = spread_rows(received[:, lay.size :], lay.size)
        extra = advanced(states, lay.rows(work, 2)[:, 0:1], lay.rows(work, 3)[:, 0:1]) + work[lay.own, span]
        total = received[:, : lay.size]
        message_ref[...] = jnp.concatenate([total, packed_rows(extra, width)], axis=1).astype(jnp.bfloat16)
        work[:width, span] = total

        @pl.when(right)
        def _():
            work[lay.enter, span] = states


def packed_shape(width, hours):
    return (width + width // 2, hours) if hours == 2 * width else (width, hours + width)


def packed(filtered, gram):
    width, hours = filtered.shape
    if hours == 2 * width:
        halves = jnp.concatenate([gram[: width // 2], gram[width // 2 :]], axis=1)
        return jnp.concatenate([filtered, halves], axis=0)
    return jnp.concatenate([filtered, gram], axis=1)


def unpacked(sums, width, hours):
    if hours == 2 * width:
        halves = sums[width:]
        return sums[:width], jnp.concatenate([halves[:, :width], halves[:, width:]], axis=0)
    return sums[:, :hours], sums[:, hours:]


def gather_kernel(lay, part, line, place_ref, slab_ref, recv_ref, _, work, *results):
    width, hours, span = lay.width, lay.hours, lay.part(part)
    place = place_ref[0]
    last_left, last_right = place == 0, place == line - 1
    outermost = (last_left | last_right) if line > 2 else False
    rounded = work[:width, span].astype(jnp.bfloat16)
    patterns = jnp.where(outermost, recv_ref[:, : lay.size], rounded)
    states = work[lay.enter, span]
    if line > 2:
        arrived = spread_rows(recv_ref[:, lay.size :].astype(jnp.float32), lay.size)
        states = jnp.where(last_right, arrived, states)

        @pl.when(outermost)
        def _():
            lost = work[:width, span] - rounded.astype(jnp.float32)
            work[:width, span] = patterns.astype(jnp.float32) + lost

    def product(value):
        return lax.dot_general(patterns, value, (((1,), (1,)), ((), ())), preferred_element_type=jnp.float32)

    cells = slab_ref.shape[1]
    slab_sums = lax.dot_general(
        patterns[:, :cells], slab_ref[...], (((1,), (1,)), ((), ())), preferred_element_type=jnp.float32
    )
    blocks = (slab_sums, product(patterns), product(doubled(states).astype(jnp.bfloat16)))
    sums = jnp.concatenate(blocks, axis=1)
    running = slice(lay.running, lay.running + hours + width + STATES)
    if part:
        sums = work[:width, running] + sums
    if part < lay.parts - 1:
        work[:width, running] = sums
        return
    sums_ref, own_ref = results
    over_states = (((1,), (1,)), ((), ()))
    filtered = [
        lax.dot_general(sums[:, :hours], work[:width, lay.filter_block(block)], over_states, precision=TOP)
        for block in range(lay.blocks)
    ]
    filtered = filtered[0] if lay.blocks == 1 else jnp.concatenate(filtered, axis=1)
    entering = jnp.dot(sums[:, hours + width :], lay.rows(work, 0)[:, :hours], precision=TOP)
    sums_ref[...] = packed(filtered + entering, sums[:, hours : hours + width])
    own_ref[...] = work[:width, pl.ds(pl.multiple_of(place * lay.own_cells, LANES), lay.own_cells)]


def inverse_factor(gram):
    width = gram.shape[0]
    row = lax.broadcasted_iota(jnp.int32, (width, width), 0)
    column = lax.broadcasted_iota(jnp.int32, (width, width), 1)
    work = jnp.concatenate([gram, jnp.where(row == column, 1.0, 0.0)], axis=1)
    tiles = [work[place : place + STATES] for place in range(0, width, STATES)]
    done = []
    for first in range(0, width, STATES):
        block = first // STATES
        spread = [
            [jnp.broadcast_to(tile[:, first + q : first + q + 1], tile.shape) for q in range(STATES)]
            for tile in tiles[block:]
        ]
        rows = [tiles[block][q : q + 1] for q in range(STATES)]
        value = [[spread[0][q][p : p + 1] for q in range(p + 1)] for p in range(STATES)]
        over, low = [None] * STATES, [[None] * STATES for _ in range(STATES)]
        for p in range(STATES):
            over[p] = 1.0 / value[p][p]
            done.append(rows[p] * lax.rsqrt(value[p][p]))
            for q in range(p + 1, STATES):
                low[q][p] = value[q][p] * over[p]
                rows[q] = rows[q] - low[q][p] * rows[p]
                for t in range(p + 1, q + 1):
                    value[q][t] = value[q][t] - low[q][p] * value[t][p]
        solved = [rows[p] * over[p] for p in range(STATES)]
        for p in reversed(range(STATES)):
            for q in range(p + 1, STATES):
                solved[p] = solved[p] - low[q][p] * solved[q]
        for place in range(block + 1, len(tiles)):
            for q in range(STATES):
                tiles[place] = tiles[place] - spread[place - block][q] * solved[q]
    return jnp.concatenate(done, axis=0)[:, width:]


def tail_kernel(basis_scale, pcs_scale, one_ref, two_ref, own_ref, basis_ref, pcs_ref):
    width = own_ref.shape[0]
    sums = one_ref[...] + two_ref[...]
    filtered, gram = unpacked(sums, width, pcs_ref.shape[1])
    inverse = inverse_factor(gram)
    pcs_ref[...] = jnp.dot(inverse * pcs_scale, filtered, precision=TOP)
    own = own_ref[...]
    own_high = own.astype(jnp.bfloat16)
    own_low = (own - own_high.astype(jnp.float32)).astype(jnp.bfloat16)
    inverse = inverse * basis_scale
    high = inverse.astype(jnp.bfloat16)
    low = (inverse - high.astype(jnp.float32)).astype(jnp.bfloat16)
    basis = jnp.dot(
        jnp.concatenate([high, high, low], axis=1),
        jnp.concatenate([own_high, own_low, own_high], axis=0),
        preferred_element_type=jnp.float32,
    )
    for group in range(basis_ref.shape[0]):
        basis_ref[group] = basis[:, group * LANES : (group + 1) * LANES]


def call(kernel, name, out_shape, *args, scalars=1, far=0, scratch=(), in_place=0, final=False):
    smem, vmem = pl.BlockSpec(memory_space=pltpu.SMEM), pl.BlockSpec(memory_space=pltpu.VMEM)
    hbm = pl.BlockSpec(memory_space=pltpu.HBM)
    count = len(args)
    keep = pltpu.with_memory_space_constraint
    args = list(args[:scalars]) + [
        keep(arg, pltpu.HBM if place < far else pltpu.VMEM) for place, arg in enumerate(args[scalars:])
    ]
    return pl.pallas_call(
        kernel,
        out_shape=out_shape if final else [pltpu.VMEM(out.shape, out.dtype) for out in out_shape],
        in_specs=[smem] * scalars + [hbm] * far + [vmem] * (count - scalars - far),
        out_specs=[vmem] * len(out_shape),
        scratch_shapes=scratch,
        input_output_aliases={count - in_place + place: place for place in range(in_place)},
        compiler_params=pltpu.CompilerParams(vmem_limit_bytes=VMEM_LIMIT),
        cost_estimate=pl.CostEstimate(flops=1, bytes_accessed=1, transcendentals=0),
        name=name,
    )(*args)


def complete(moves, size, cores, both):
    moves = moves + [(target, source) for source, target in moves] if both else moves
    used = {device for move in moves for device in move}
    full = [(source * cores + core, target * cores + core) for source, target in moves for core in range(cores)]
    other = 1 if cores % 2 == 0 else 0
    idle = [device * cores + core for device in range(size) if device not in used for core in range(cores)]
    return full + [(device, device ^ other) for device in idle]


def local(slab, start, sections):
    hours, cells = slab.shape
    width = start.shape[1]
    line = lax.axis_size("tm")
    half = line // 2
    parts = PARTS
    lay = Layout(hours, cells, width, parts, line)
    f32, bf16 = jnp.float32, jnp.bfloat16
    shape = jax.ShapeDtypeStruct
    place = lax.axis_index("tm").astype(jnp.int32).reshape(1)
    work_shape = shape(lay.shape, f32)
    message_shape = shape((width, lay.size + extra_columns(lay.size, width)), bf16)
    scratch = [
        pltpu.VMEM(slab.shape, bf16), pltpu.VMEM((width, hours), bf16), pltpu.SMEM((2, 3), f32), pltpu.SemaphoreType.DMA((3,)),
    ]
    inputs = (place, sections.T, slab, start.T)
    work, message = call(
        functools.partial(head_kernel, lay, line), "head", [work_shape, message_shape], *inputs, far=3, scratch=scratch
    )
    work, *messages = call(
        functools.partial(rest_kernel, lay, line), "rest", [work_shape] + [message_shape] * (parts - 1), *inputs, work,
        far=3, in_place=1, scratch=[*scratch, pltpu.SemaphoreType.DMA((parts - 1,))],
    )
    messages = [message, *messages]
    results = [work_shape, message_shape]

    def inward_moves(hop):
        return [(hop, hop + 1), (line - 1 - hop, line - 2 - hop)]

    def send(message, moves, both=False):
        return lax.ppermute(message, ("tm", "lon"), complete(moves, line, lax.axis_size("lon"), both))

    def gather(part, block, work):
        shapes = [work_shape]
        if part == parts - 1:
            shapes += [shape(packed_shape(width, hours), f32), shape((width, lay.own_cells), f32)]
        kernel = functools.partial(gather_kernel, lay, part, line)
        return call(kernel, "gather", shapes, place, slab[:, lay.real(part)], block, work, in_place=1)

    def inward(part, hop, block, work):
        kernel = functools.partial(inward_kernel, lay, part, hop, line)
        return call(kernel, "inward", results, place, block, work, in_place=1)

    def middle(part, block, work, *message):
        kernel = functools.partial(middle_kernel, lay, part, line)
        return call(kernel, "middle", results, place, block, work, *message, in_place=1 + len(message))

    middle_moves = [(half - 1, half), (half, half - 1)]
    if half == 2:
        crossing = [send(message, inward_moves(0), True) for message in messages[:LAG]]
        between = [None] * parts
        for step in range(parts + LAG):
            if step < parts:
                work, message = inward(step, 0, crossing[step], work)
                between[step] = send(message, middle_moves)
            if step >= LAG:
                work, *rest = gather(step - LAG, crossing[step], work)
            if 1 <= step <= parts:
                later = step - 1 + LAG
                swapped_in = [messages[later]] if later < parts else []
                work, message = middle(step - 1, between[step - 1], work, *swapped_in)
                crossing.append(send(message, inward_moves(0), True))
    else:
        arriving = [send(message, inward_moves(0)) if half > 1 else message for message in messages]
        for part in range(parts):
            message, block = messages[part], arriving[part]
            for hop in range(half - 1):
                work, message = inward(part, hop, block, work)
                if hop < half - 2:
                    block = send(message, inward_moves(hop + 1))
            block = send(message, middle_moves)
            work, message = middle(part, block, work)
            for hop in range(half - 1):
                block = send(message, [(target, source) for source, target in inward_moves(half - 2 - hop)])
                if hop < half - 2:
                    kernel = functools.partial(outward_kernel, lay, part, hop, line)
                    work, message = call(kernel, "outward", results, place, block, work, in_place=1)
            work, *rest = gather(part, block, work)
    running, own = rest

    steps = []
    for axis in ("lon", "lat"):
        size, stride = lax.axis_size(axis), 1
        while stride < size:
            steps.append((axis, [(i, i ^ stride) for i in range(size)]))
            stride *= 2
    for axis, moves in steps[:-1]:
        running = running + lax.ppermute(running, axis, moves)
    other = lax.ppermute(running, *steps[-1])

    part_cells = lay.own_cells
    cells_all = cells * lax.axis_size("lat") * lax.axis_size("lon")
    basis, pcs = call(
        functools.partial(tail_kernel, math.sqrt(cells_all), math.sqrt(hours * line / cells_all)), "tail",
        [shape((part_cells // LANES, width, LANES), f32), shape((width, hours), f32)],
        running, other, own, scalars=0, final=True,
    )
    return (basis, pcs.T)


def solution(mesh):
    return jax.shard_map(
        local,
        mesh=mesh,
        in_specs=(P("tm", ("lat", "lon")), P("tm", None), P()),
        out_specs=(P(("lat", "lon", "tm"), None, None), P("tm", None)),
        check_vma=False,
    )
```

```python
import functools
import math

import jax
import jax.numpy as jnp
from jax import lax
from jax.experimental import pallas as pl
from jax.experimental.pallas import tpu as pltpu
from jax.sharding import PartitionSpec as P

LANES = 128
STATES = 8
TOP = lax.Precision.HIGHEST
VMEM_LIMIT = 8 * 1024 * 1024
SIZES = (11, 11, 11, 11, 12, 8)
LAG = 3


def row_pairs(first, second):
    row = lax.broadcasted_iota(jnp.int32, (STATES, LANES), 0)
    return jnp.where(row % 4 < 2, first, second)


def swapped(value):
    row = lax.broadcasted_iota(jnp.int32, value.shape, 0)
    return jnp.where(row % 2 == 0, pltpu.roll(value, STATES - 1, 0), pltpu.roll(value, 1, 0))


def tables(section_ref, hours):
    shape = (STATES, LANES)
    radius, angle, amplitude = (row_pairs(section_ref[0, i], section_ref[1, i]) for i in range(3))
    hour = lax.broadcasted_iota(jnp.int32, shape, 1).astype(jnp.float32)
    imaginary = lax.broadcasted_iota(jnp.int32, shape, 0) % 2 == 1
    sign = jnp.where(imaginary, 1.0, -1.0)
    drive = amplitude * jnp.sqrt(1.0 - radius * radius)
    back = 1.0 / (radius * radius)
    gain_re = drive * (1.0 + back)
    gain_im = -drive * (1.0 - back) * jnp.cos(angle) / jnp.sin(angle)
    log_radius = jnp.log(radius)

    def power(n):
        turn = n * angle
        return jnp.exp(n * log_radius) * jnp.where(imaginary, jnp.sin(turn), jnp.cos(turn))

    ahead = power(hour)
    outgoing = -sign * (gain_re * ahead + sign * gain_im * swapped(ahead))
    inverse, incoming = power(-hour), power(hours - hour)
    lam = power(jnp.full(shape, hours, jnp.float32))
    keep = jnp.where(imaginary, swapped(lam), lam)
    swap = sign * jnp.where(imaginary, lam, swapped(lam))
    diagonal = drive[0:1, 0:1] + drive[2:3, 0:1]
    return outgoing, incoming, inverse, keep, swap, diagonal


def doubled(value):
    rounded = value.astype(jnp.bfloat16).astype(jnp.float32)
    row = lax.broadcasted_iota(jnp.int32, value.shape, 0)
    return jnp.where(row < STATES // 2, rounded, value - rounded)


def joined(value):
    return value + pltpu.roll(value, STATES // 2, 0)


def extra_columns(cells, width):
    tiles = -(-cells // (2 * LANES))
    return -(-tiles // (width // STATES)) * LANES


def packed_rows(rows, width, columns):
    cells = rows.shape[1]
    upper = lax.broadcasted_iota(jnp.int32, (STATES, LANES), 0) < STATES // 2
    zero = jnp.zeros((STATES, LANES), jnp.float32)
    groups = [rows[:, start : start + LANES] for start in range(0, cells, LANES)] + [zero]
    tiles = [jnp.where(upper, groups[i], groups[i + 1]) for i in range(0, len(groups) - 1, 2)]
    tall = width // STATES
    tiles += [zero] * (tall * columns // LANES - len(tiles))
    blocks = [jnp.concatenate(tiles[i : i + tall], axis=0) for i in range(0, len(tiles), tall)]
    return blocks[0] if len(blocks) == 1 else jnp.concatenate(blocks, axis=1)


def spread_rows(block, cells):
    upper = lax.broadcasted_iota(jnp.int32, (STATES, LANES), 0) < STATES // 2
    tall = block.shape[0] // STATES
    groups = []
    for group in range(cells // LANES):
        column, tile = divmod(group // 2, tall)
        value = block[tile * STATES : (tile + 1) * STATES, column * LANES : (column + 1) * LANES]
        groups.append(joined(jnp.where(upper if group % 2 == 0 else jnp.logical_not(upper), value, 0.0)))
    return jnp.concatenate(groups, axis=1)


def advanced(value, keep, swap):
    return keep * value + swap * swapped(value)


def split(value):
    high = value.astype(jnp.bfloat16)
    return high, (value - high.astype(jnp.float32)).astype(jnp.bfloat16)


def exact_dot(short, value):
    high, low = split(value)
    return jnp.dot(short, high, preferred_element_type=jnp.float32) + jnp.dot(
        short, low, preferred_element_type=jnp.float32
    )


def stacked_dot(left, right, axis):
    left_high, left_low = split(left)
    right_high, right_low = split(right)
    return lax.dot_general(
        jnp.concatenate([left_high, left_high, left_low], axis=1),
        jnp.concatenate([right_high, right_low, right_high], axis=axis),
        (((1,), (axis,)), ((), ())),
        preferred_element_type=jnp.float32,
    )


def outer(columns, rows):
    total = columns[:, 0:1] * rows[0:1, :]
    for k in range(1, STATES // 2):
        total = total + columns[:, k : k + 1] * rows[k : k + 1, :]
    return total


class Layout:
    def __init__(self, hours, cells, width, sizes, line):
        self.hours, self.width, self.sizes, self.parts = hours, width, sizes, len(sizes)
        self.extra = extra_columns(max(sizes), width)
        self.own_cells = cells // line
        self.own = slice(width, width + STATES)
        self.out = slice(width + STATES, width + 2 * STATES)
        self.enter = slice(width + 2 * STATES, width + 3 * STATES)
        self.blocks = hours // width
        self.filter = cells
        self.table = self.filter + self.blocks * LANES
        self.weights = self.table + LANES
        self.running = self.weights + LANES
        self.columns = self.running + LANES * (-(-(hours + width + STATES) // LANES))
        self.shape = (width + 3 * STATES, self.columns)

    def part(self, part):
        start = sum(self.sizes[:part])
        return slice(start, start + self.sizes[part])

    def take(self, message_ref, part):
        value = message_ref[...].astype(jnp.float32)
        size = self.sizes[part]
        return value[:, :size], spread_rows(value[:, value.shape[1] - self.extra :], size)

    def put(self, message_ref, patterns, states):
        packed_states = packed_rows(states, self.width, self.extra)
        room = message_ref.shape[1] - self.extra - patterns.shape[1]
        pieces = [patterns, jnp.zeros((self.width, room), jnp.float32), packed_states] if room else [patterns, packed_states]
        message_ref[...] = jnp.concatenate(pieces, axis=1).astype(jnp.bfloat16)

    def weights_row(self, work, part):
        handed = self.rows(work, 1)
        return jnp.concatenate([handed, jnp.zeros((STATES, self.sizes[part] - LANES), jnp.float32)], axis=1)

    def rows(self, work, place):
        return work[place * STATES : (place + 1) * STATES, self.table : self.table + LANES]

    def filter_block(self, block):
        start = self.filter + block * LANES
        return slice(start, start + self.hours)


def add_part(lay, part, left, slab_ref, work, message_ref):
    width, span = lay.width, lay.part(part)
    weights = work[: width + STATES, lay.weights : lay.weights + lay.hours]
    high, low = split(weights)
    block = slab_ref[:, span]
    total = jnp.dot(high, block, preferred_element_type=jnp.float32) + jnp.dot(
        low, block, preferred_element_type=jnp.float32
    )
    work[: width + STATES, span] = total
    if message_ref is not None:
        lay.put(message_ref, total[:width], jnp.where(left, total[width:], lay.weights_row(work, part)))


def begin(lay, left, section_hbm, slab_hbm, start_hbm, work, message_ref, slab_ref, start_ref, section_ref, arrived):
    width, hours = lay.width, lay.hours
    copies = [
        pltpu.make_async_copy(section_hbm, section_ref, arrived.at[0]),
        pltpu.make_async_copy(start_hbm, start_ref, arrived.at[1]),
        pltpu.make_async_copy(slab_hbm.at[:, lay.part(0)], slab_ref.at[:, lay.part(0)], arrived.at[2]),
    ]
    for copy in copies:
        copy.start()
    copies[0].wait()
    outgoing, incoming, inverse, keep, swap, diagonal = tables(section_ref, hours)
    later = lax.broadcasted_iota(jnp.int32, (hours, hours), 0)
    earlier = lax.broadcasted_iota(jnp.int32, (hours, hours), 1)
    columns = jnp.transpose(outgoing[:, :hours])
    full = outer(columns, inverse[:, :hours])
    full = jnp.where(later > earlier, full, jnp.where(later == earlier, diagonal, 0.0))
    copies[1].wait()
    start = start_ref[...]
    work[:width, lay.weights : lay.weights + hours] = exact_dot(start, full)
    work[width : width + STATES, lay.weights : lay.weights + hours] = incoming[:, :hours]
    handed = jnp.transpose(exact_dot(start, columns))
    handed = jnp.concatenate([handed, jnp.zeros((STATES, LANES - width), jnp.float32)], axis=1)
    table = work.at[:, lay.table : lay.table + LANES]
    table[STATES : 2 * STATES, :] = handed
    copies[2].wait()
    add_part(lay, 0, left, slab_ref, work, message_ref)
    for block in range(lay.blocks):
        work[:width, lay.filter_block(block)] = full[block * width : (block + 1) * width]
    for place, value in ((0, outgoing), (2, keep), (3, swap)):
        table[place * STATES : (place + 1) * STATES, :] = value


def head_kernel(lay, line, place_ref, section_hbm, slab_hbm, start_hbm, work, message_ref, *scratch):
    place = place_ref[0]

    @pl.when((place == 0) | (place == line - 1))
    def _():
        begin(lay, place < line // 2, section_hbm, slab_hbm, start_hbm, work, message_ref, *scratch)


def second_kernel(lay, line, place_ref, slab_hbm, _, work, message_ref, slab_ref, arrived):
    place = place_ref[0]

    @pl.when((place == 0) | (place == line - 1))
    def _():
        span = lay.part(1)
        copy = pltpu.make_async_copy(slab_hbm.at[:, span], slab_ref.at[:, span], arrived)
        copy.start()
        copy.wait()
        add_part(lay, 1, place < line // 2, slab_ref, work, message_ref)


def rest_kernel(lay, line, place_ref, section_hbm, slab_hbm, start_hbm, _, work, *refs):
    messages, scratch = refs[: lay.parts - 2], refs[lay.parts - 2 :]
    slab_ref, landed = scratch[0], scratch[-1]
    place = place_ref[0]
    left = place < line // 2
    inner = (place != 0) & (place != line - 1)
    copies = []
    for part in range(1, lay.parts):
        span = lay.part(part)
        copies.append(pltpu.make_async_copy(slab_hbm.at[:, span], slab_ref.at[:, span], landed.at[part - 1]))
        copies[-1].start()
    work[lay.enter, : lay.filter] = jnp.zeros((STATES, lay.filter), jnp.float32)

    @pl.when(inner)
    def _():
        begin(lay, left, section_hbm, slab_hbm, start_hbm, work, None, *scratch[:-1])

    copies[0].wait()

    @pl.when(inner)
    def _():
        add_part(lay, 1, left, slab_ref, work, None)

    for part in range(2, lay.parts):
        copies[part - 1].wait()
        add_part(lay, part, left, slab_ref, work, messages[part - 2])


def column_of(rows, width):
    return jnp.transpose(rows[:, :LANES])[:width]


def inward_kernel(lay, part, hop, line, place_ref, recv_ref, _, work, message_ref):
    width, span = lay.width, lay.part(part)
    place = place_ref[0]
    left = place == hop + 1

    @pl.when(left | (place == line - 2 - hop))
    def _():
        received, states = lay.take(recv_ref, part)
        states_own = work[lay.own, span]
        columns = column_of(jnp.where(left, lay.rows(work, 1), states[:, :LANES]), width)
        rows = jnp.where(left, states, states_own)
        total = received + work[:width, span] + outer(columns, rows)
        swap = lay.rows(work, 3)[:, 0:1]
        extra = advanced(states, lay.rows(work, 2)[:, 0:1], jnp.where(left, swap, -swap))
        extra = extra + jnp.where(left, states_own, lay.weights_row(work, part))
        lay.put(message_ref, total, extra)
        work[:width, span] = total
        work[lay.out, span] = extra
        work[lay.enter, span] = jnp.where(left, states, 0.0)


def middle_kernel(lay, part, line, place_ref, recv_ref, *refs):
    work, message_ref = refs[-2:]
    width, span = lay.width, lay.part(part)
    place = place_ref[0]
    left = place == line // 2 - 1

    @pl.when(left | (place == line // 2))
    def _():
        received, states = lay.take(recv_ref, part)
        handed = work[lay.out, span]
        columns = column_of(jnp.where(left, states[:, :LANES], handed[:, :LANES]), width)
        total = received + work[:width, span] + outer(columns, jnp.where(left, handed, states))
        extra = advanced(states, lay.rows(work, 2)[:, 0:1], lay.rows(work, 3)[:, 0:1]) + work[lay.own, span]
        lay.put(message_ref, total, extra)
        work[:width, span] = total

        @pl.when(jnp.logical_not(left))
        def _():
            work[lay.enter, span] = states


def outward_kernel(lay, part, hop, line, place_ref, recv_ref, _, work, message_ref):
    width, span = lay.width, lay.part(part)
    place = place_ref[0]
    right = place == line // 2 + 1 + hop

    @pl.when(right | (place == line // 2 - 2 - hop))
    def _():
        total, states = lay.take(recv_ref, part)
        extra = advanced(states, lay.rows(work, 2)[:, 0:1], lay.rows(work, 3)[:, 0:1]) + work[lay.own, span]
        lay.put(message_ref, total, extra)
        work[:width, span] = total

        @pl.when(right)
        def _():
            work[lay.enter, span] = states


def packed_shape(width, hours):
    return (width + width // 2, hours) if hours == 2 * width else (width, hours + width)


def packed(filtered, gram):
    width, hours = filtered.shape
    if hours == 2 * width:
        halves = jnp.concatenate([gram[: width // 2], gram[width // 2 :]], axis=1)
        return jnp.concatenate([filtered, halves], axis=0)
    return jnp.concatenate([filtered, gram], axis=1)


def unpacked(sums, width, hours):
    if hours == 2 * width:
        halves = sums[width:]
        return sums[:width], jnp.concatenate([halves[:, :width], halves[:, width:]], axis=0)
    return sums[:, :hours], sums[:, hours:]


def gather_kernel(lay, part, line, place_ref, slab_ref, recv_ref, _, work, *results):
    width, hours, span = lay.width, lay.hours, lay.part(part)
    place = place_ref[0]
    last_left, last_right = place == 0, place == line - 1
    outermost = (last_left | last_right) if line > 2 else False
    rounded = work[:width, span].astype(jnp.bfloat16)
    patterns = jnp.where(outermost, recv_ref[:, : lay.sizes[part]], rounded)
    states = work[lay.enter, span]
    if line > 2:
        states = jnp.where(last_right, lay.take(recv_ref, part)[1], states)

        @pl.when(outermost)
        def _():
            lost = work[:width, span] - rounded.astype(jnp.float32)
            work[:width, span] = patterns.astype(jnp.float32) + lost

    def product(value):
        return lax.dot_general(patterns, value, (((1,), (1,)), ((), ())), preferred_element_type=jnp.float32)

    blocks = (product(slab_ref[...]), product(patterns), product(doubled(states).astype(jnp.bfloat16)))
    sums = jnp.concatenate(blocks, axis=1)
    running = slice(lay.running, lay.running + hours + width + STATES)
    if part:
        sums = work[:width, running] + sums
    if part < lay.parts - 1:
        work[:width, running] = sums
        return
    (sums_ref,) = results
    filtered = [
        stacked_dot(sums[:, :hours], work[:width, lay.filter_block(block)], 1)
        for block in range(lay.blocks)
    ]
    filtered = filtered[0] if lay.blocks == 1 else jnp.concatenate(filtered, axis=1)
    entering = jnp.dot(sums[:, hours + width :], lay.rows(work, 0)[:, :hours], precision=TOP)
    sums_ref[...] = packed(filtered + entering, sums[:, hours : hours + width])


def own_kernel(lay, place_ref, work, owns_ref):
    start = pl.multiple_of(place_ref[0] * lay.own_cells, LANES)
    high, low = split(work[: lay.width, pl.ds(start, lay.own_cells)])
    owns_ref[...] = jnp.concatenate([high, low, high], axis=0)


def inverse_factor(gram):
    width = gram.shape[0]
    row = lax.broadcasted_iota(jnp.int32, (width, width), 0)
    column = lax.broadcasted_iota(jnp.int32, (width, width), 1)
    work = jnp.concatenate([gram, jnp.where(row == column, 1.0, 0.0)], axis=1)
    tiles = [work[place : place + STATES] for place in range(0, width, STATES)]
    done = []
    for first in range(0, width, STATES):
        block = first // STATES
        spread = [
            [jnp.broadcast_to(tile[:, first + q : first + q + 1], tile.shape) for q in range(STATES)]
            for tile in tiles[block:]
        ]
        rows = [tiles[block][q : q + 1] for q in range(STATES)]
        value = [[spread[0][q][p : p + 1] for q in range(p + 1)] for p in range(STATES)]
        for p in range(0, STATES, 2):
            one, two = rows[p], rows[p + 1]
            a, b, d = value[p][p], value[p + 1][p], value[p + 1][p + 1]
            over = 1.0 / (a * d - b * b)
            ratio = b / a
            done.append(one * lax.rsqrt(a))
            done.append((two - ratio * one) * lax.rsqrt(d - ratio * b))
            for q in range(p + 2, STATES):
                x, y = value[q][p], value[q][p + 1]
                first_part, second_part = (x * d - y * b) * over, (y * a - x * b) * over
                for t in range(p + 2, q + 1):
                    value[q][t] = value[q][t] - (first_part * value[t][p] + second_part * value[t][p + 1])
                rows[q] = rows[q] - (first_part * one + second_part * two)
                for low in spread[1:]:
                    low[q] = low[q] - (first_part * low[p] + second_part * low[p + 1])
            one, two = (d * one - b * two) * over, (a * two - b * one) * over
            for place, low in enumerate(spread[1:], block + 1):
                tiles[place] = tiles[place] - (low[p] * one + low[p + 1] * two)
    return jnp.concatenate(done, axis=0)[:, width:]


def tail_kernel(basis_scale, pcs_scale, *refs):
    *shares, owns_ref, basis_ref, pcs_ref = refs
    width = basis_ref.shape[1]
    shares = [share[...] for share in shares]
    while len(shares) > 1:
        shares = [one + two for one, two in zip(shares[::2], shares[1::2])]
    sums = shares[0]
    filtered, gram = unpacked(sums, width, pcs_ref.shape[1])
    inverse = inverse_factor(gram)
    pcs_ref[...] = stacked_dot(inverse * pcs_scale, filtered, 0)
    high, low = split(inverse * basis_scale)
    inverses = jnp.concatenate([high, high, low], axis=1)
    basis = jnp.dot(inverses, owns_ref[...], preferred_element_type=jnp.float32)
    for group in range(basis_ref.shape[0]):
        basis_ref[group] = basis[:, group * LANES : (group + 1) * LANES]


def call(kernel, name, out_shape, *args, scalars=1, far=0, scratch=(), in_place=0, final=False):
    smem, vmem = pl.BlockSpec(memory_space=pltpu.SMEM), pl.BlockSpec(memory_space=pltpu.VMEM)
    hbm = pl.BlockSpec(memory_space=pltpu.HBM)
    count = len(args)
    keep = pltpu.with_memory_space_constraint
    args = list(args[:scalars]) + [
        keep(arg, pltpu.HBM if place < far else pltpu.VMEM) for place, arg in enumerate(args[scalars:])
    ]
    return pl.pallas_call(
        kernel,
        out_shape=out_shape if final else [pltpu.VMEM(out.shape, out.dtype) for out in out_shape],
        in_specs=[smem] * scalars + [hbm] * far + [vmem] * (count - scalars - far),
        out_specs=[vmem] * len(out_shape),
        scratch_shapes=scratch,
        input_output_aliases={count - in_place + place: place for place in range(in_place)},
        compiler_params=pltpu.CompilerParams(vmem_limit_bytes=VMEM_LIMIT),
        cost_estimate=pl.CostEstimate(flops=1, bytes_accessed=1, transcendentals=0),
        name=name,
    )(*args)


def complete(moves, size, cores, both):
    moves = moves + [(target, source) for source, target in moves] if both else moves
    used = {device for move in moves for device in move}
    full = [(source * cores + core, target * cores + core) for source, target in moves for core in range(cores)]
    other = 1 if cores % 2 == 0 else 0
    idle = [device * cores + core for device in range(size) if device not in used for core in range(cores)]
    return full + [(device, device ^ other) for device in idle]


def local(slab, start, sections):
    hours, cells = slab.shape
    width = start.shape[1]
    line = lax.axis_size("tm")
    half = line // 2
    groups, parts = cells // LANES, len(SIZES)
    ends = [groups * sum(SIZES[:part]) // sum(SIZES) * LANES for part in range(parts + 1)]
    sizes = [end - start for start, end in zip(ends, ends[1:])]
    lay = Layout(hours, cells, width, sizes, line)
    f32, bf16 = jnp.float32, jnp.bfloat16
    shape = jax.ShapeDtypeStruct
    place = lax.axis_index("tm").astype(jnp.int32).reshape(1)
    work_shape = shape(lay.shape, f32)

    def message_shape(room):
        return shape((width, room + lay.extra), bf16)

    def room(exchange):
        held = [part for part in (exchange, exchange - LAG) if 0 <= part < parts]
        return max(sizes[part] for part in held[: 2 if half == 2 else 1])

    first, *others = [message_shape(room(part)) for part in range(parts)]
    scratch = [
        pltpu.VMEM(slab.shape, bf16), pltpu.VMEM((width, hours), bf16), pltpu.SMEM((2, 3), f32), pltpu.SemaphoreType.DMA((3,)),
    ]
    inputs = (place, sections.T, slab, start.T)
    work, message = call(
        functools.partial(head_kernel, lay, line), "head", [work_shape, first], *inputs, far=3, scratch=scratch
    )
    work, second = call(
        functools.partial(second_kernel, lay, line), "second", [work_shape, others[0]], place, slab, work, far=1,
        in_place=1, scratch=[pltpu.VMEM(slab.shape, bf16), pltpu.SemaphoreType.DMA(())],
    )
    work, *messages = call(
        functools.partial(rest_kernel, lay, line), "rest", [work_shape] + others[1:], *inputs, work,
        far=3, in_place=1, scratch=[*scratch, pltpu.SemaphoreType.DMA((parts - 1,))],
    )
    messages = [message, second, *messages]

    def results(part, exchange=None):
        return [work_shape, message_shape(sizes[part] if exchange is None else room(exchange))]

    def inward_moves(hop):
        return [(hop, hop + 1), (line - 1 - hop, line - 2 - hop)]

    def send(message, moves, both=False):
        return lax.ppermute(message, ("tm", "lon"), complete(moves, line, lax.axis_size("lon"), both))

    def gather(part, block, work):
        shapes = [work_shape]
        if part == parts - 1:
            shapes += [shape(packed_shape(width, hours), f32)]
        kernel = functools.partial(gather_kernel, lay, part, line)
        return call(kernel, "gather", shapes, place, slab[:, lay.part(part)], block, work, in_place=1)

    def inward(part, hop, block, work):
        kernel = functools.partial(inward_kernel, lay, part, hop, line)
        return call(kernel, "inward", results(part), place, block, work, in_place=1)

    def middle(part, block, work, *message, exchange=None):
        kernel = functools.partial(middle_kernel, lay, part, line)
        return call(kernel, "middle", results(part, exchange), place, block, work, *message, in_place=1 + len(message))

    middle_moves = [(half - 1, half), (half, half - 1)]
    if half == 2:
        crossing = [send(message, inward_moves(0), True) for message in messages[:LAG]]
        between = [None] * parts
        for step in range(parts + LAG):
            if step < parts:
                work, message = inward(step, 0, crossing[step], work)
                between[step] = send(message, middle_moves)
            if step >= LAG:
                work, *rest = gather(step - LAG, crossing[step], work)
            if 1 <= step <= parts:
                later = step - 1 + LAG
                swapped_in = [messages[later]] if later < parts else []
                work, message = middle(step - 1, between[step - 1], work, *swapped_in, exchange=later)
                crossing.append(send(message, inward_moves(0), True))
    else:
        arriving = [send(message, inward_moves(0)) if half > 1 else message for message in messages]
        for part in range(parts):
            message, block = messages[part], arriving[part]
            for hop in range(half - 1):
                work, message = inward(part, hop, block, work)
                if hop < half - 2:
                    block = send(message, inward_moves(hop + 1))
            block = send(message, middle_moves)
            work, message = middle(part, block, work)
            for hop in range(half - 1):
                block = send(message, [(target, source) for source, target in inward_moves(half - 2 - hop)])
                if hop < half - 2:
                    kernel = functools.partial(outward_kernel, lay, part, hop, line)
                    work, message = call(kernel, "outward", results(part), place, block, work, in_place=1)
            work, *rest = gather(part, block, work)
    (running,) = rest
    kernel = functools.partial(own_kernel, lay)
    (owns,) = call(kernel, "own", [shape((3 * width, lay.own_cells), bf16)], place, work)

    cores, bands = lax.axis_size("lon"), lax.axis_size("lat")
    stride = 1
    while stride < cores:
        running = running + lax.ppermute(running, "lon", [(i, i ^ stride) for i in range(cores)])
        stride *= 2
    shares = [running]
    shares += [lax.ppermute(running, "lat", [(i, i ^ way) for i in range(bands)]) for way in range(1, bands)]

    cells_all = cells * lax.axis_size("lat") * lax.axis_size("lon")
    basis, pcs = call(
        functools.partial(tail_kernel, math.sqrt(cells_all), math.sqrt(hours * line / cells_all)), "tail",
        [shape((lay.own_cells // LANES, width, LANES), f32), shape((width, hours), f32)],
        *shares, owns, scalars=0, final=True,
    )
    return (basis, pcs.T)


def solution(mesh):
    return jax.shard_map(
        local,
        mesh=mesh,
        in_specs=(P("tm", ("lat", "lon")), P("tm", None), P()),
        out_specs=(P(("lat", "lon", "tm"), None, None), P("tm", None)),
        check_vma=False,
    )
```

```python
import functools
import math

import jax
import jax.numpy as jnp
from jax import lax
from jax.experimental import pallas as pl
from jax.experimental.pallas import tpu as pltpu
from jax.sharding import PartitionSpec as P

LANES = 128
STATES = 8
TOP = lax.Precision.HIGHEST
VMEM_LIMIT = 8 * 1024 * 1024
SIZES = (11, 11, 11, 11, 12, 8)
LAG = 3


def row_pairs(first, second):
    row = lax.broadcasted_iota(jnp.int32, (STATES, LANES), 0)
    return jnp.where(row % 4 < 2, first, second)


def swapped(value):
    row = lax.broadcasted_iota(jnp.int32, value.shape, 0)
    return jnp.where(row % 2 == 0, pltpu.roll(value, STATES - 1, 0), pltpu.roll(value, 1, 0))


def tables(section_ref, hours):
    shape = (STATES, LANES)
    radius, angle, amplitude = (row_pairs(section_ref[0, i], section_ref[1, i]) for i in range(3))
    hour = lax.broadcasted_iota(jnp.int32, shape, 1).astype(jnp.float32)
    imaginary = lax.broadcasted_iota(jnp.int32, shape, 0) % 2 == 1
    sign = jnp.where(imaginary, 1.0, -1.0)
    drive = amplitude * jnp.sqrt(1.0 - radius * radius)
    back = 1.0 / (radius * radius)
    gain_re = drive * (1.0 + back)
    gain_im = -drive * (1.0 - back) * jnp.cos(angle) / jnp.sin(angle)
    log_radius = jnp.log(radius)

    def power(n):
        turn = n * angle
        return jnp.exp(n * log_radius) * jnp.where(imaginary, jnp.sin(turn), jnp.cos(turn))

    ahead = power(hour)
    outgoing = -sign * (gain_re * ahead + sign * gain_im * swapped(ahead))
    inverse, incoming = power(-hour), power(hours - hour)
    lam = power(jnp.full(shape, hours, jnp.float32))
    keep = jnp.where(imaginary, swapped(lam), lam)
    swap = sign * jnp.where(imaginary, lam, swapped(lam))
    diagonal = drive[0:1, 0:1] + drive[2:3, 0:1]
    return outgoing, incoming, inverse, keep, swap, diagonal


def doubled(value):
    rounded = value.astype(jnp.bfloat16).astype(jnp.float32)
    row = lax.broadcasted_iota(jnp.int32, value.shape, 0)
    return jnp.where(row < STATES // 2, rounded, value - rounded)


def joined(value):
    return value + pltpu.roll(value, STATES // 2, 0)


def extra_columns(cells, width):
    tiles = -(-cells // (2 * LANES))
    return -(-tiles // (width // STATES)) * LANES


def packed_rows(rows, width, columns):
    cells = rows.shape[1]
    upper = lax.broadcasted_iota(jnp.int32, (STATES, LANES), 0) < STATES // 2
    zero = jnp.zeros((STATES, LANES), jnp.float32)
    groups = [rows[:, start : start + LANES] for start in range(0, cells, LANES)] + [zero]
    tiles = [jnp.where(upper, groups[i], groups[i + 1]) for i in range(0, len(groups) - 1, 2)]
    tall = width // STATES
    tiles += [zero] * (tall * columns // LANES - len(tiles))
    blocks = [jnp.concatenate(tiles[i : i + tall], axis=0) for i in range(0, len(tiles), tall)]
    return blocks[0] if len(blocks) == 1 else jnp.concatenate(blocks, axis=1)


def spread_rows(block, cells):
    upper = lax.broadcasted_iota(jnp.int32, (STATES, LANES), 0) < STATES // 2
    tall = block.shape[0] // STATES
    groups = []
    for group in range(cells // LANES):
        column, tile = divmod(group // 2, tall)
        value = block[tile * STATES : (tile + 1) * STATES, column * LANES : (column + 1) * LANES]
        groups.append(joined(jnp.where(upper if group % 2 == 0 else jnp.logical_not(upper), value, 0.0)))
    return jnp.concatenate(groups, axis=1)


def advanced(value, keep, swap):
    return keep * value + swap * swapped(value)


def split(value):
    high = value.astype(jnp.bfloat16)
    return high, (value - high.astype(jnp.float32)).astype(jnp.bfloat16)


def exact_dot(short, value):
    high, low = split(value)
    return jnp.dot(short, high, preferred_element_type=jnp.float32) + jnp.dot(
        short, low, preferred_element_type=jnp.float32
    )


def stacked_dot(left, right, axis):
    left_high, left_low = split(left)
    right_high, right_low = split(right)
    return lax.dot_general(
        jnp.concatenate([left_high, left_high, left_low], axis=1),
        jnp.concatenate([right_high, right_low, right_high], axis=axis),
        (((1,), (axis,)), ((), ())),
        preferred_element_type=jnp.float32,
    )


def outer(columns, rows):
    total = columns[:, 0:1] * rows[0:1, :]
    for k in range(1, STATES // 2):
        total = total + columns[:, k : k + 1] * rows[k : k + 1, :]
    return total


class Layout:
    def __init__(self, hours, cells, width, sizes, line):
        self.hours, self.width, self.sizes, self.parts = hours, width, sizes, len(sizes)
        self.extra = extra_columns(max(sizes), width)
        self.own_cells = cells // line
        self.own = slice(width, width + STATES)
        self.out = slice(width + STATES, width + 2 * STATES)
        self.enter = slice(width + 2 * STATES, width + 3 * STATES)
        self.blocks = hours // width
        self.filter = cells
        self.table = self.filter + self.blocks * LANES
        self.weights = self.table + LANES
        self.running = self.weights + LANES
        self.columns = self.running + LANES * (-(-(hours + width + STATES) // LANES))
        self.shape = (width + 3 * STATES, self.columns)

    def part(self, part):
        start = sum(self.sizes[:part])
        return slice(start, start + self.sizes[part])

    def take(self, message_ref, part):
        value = message_ref[...].astype(jnp.float32)
        size = self.sizes[part]
        return value[:, :size], spread_rows(value[:, value.shape[1] - self.extra :], size)

    def put(self, message_ref, patterns, states):
        packed_states = packed_rows(states, self.width, self.extra)
        room = message_ref.shape[1] - self.extra - patterns.shape[1]
        pieces = [patterns, jnp.zeros((self.width, room), jnp.float32), packed_states] if room else [patterns, packed_states]
        message_ref[...] = jnp.concatenate(pieces, axis=1).astype(jnp.bfloat16)

    def weights_row(self, work, part):
        handed = self.rows(work, 1)
        return jnp.concatenate([handed, jnp.zeros((STATES, self.sizes[part] - LANES), jnp.float32)], axis=1)

    def rows(self, work, place):
        return work[place * STATES : (place + 1) * STATES, self.table : self.table + LANES]

    def filter_block(self, block):
        start = self.filter + block * LANES
        return slice(start, start + self.hours)


def add_part(lay, part, left, slab_ref, work, message_ref):
    width, span = lay.width, lay.part(part)
    weights = work[: width + STATES, lay.weights : lay.weights + lay.hours]
    high, low = split(weights)
    block = slab_ref[:, span]
    total = jnp.dot(high, block, preferred_element_type=jnp.float32) + jnp.dot(
        low, block, preferred_element_type=jnp.float32
    )
    work[: width + STATES, span] = total
    if message_ref is not None:
        lay.put(message_ref, total[:width], jnp.where(left, total[width:], lay.weights_row(work, part)))


def begin(lay, left, section_hbm, slab_hbm, start_hbm, work, message_ref, slab_ref, start_ref, section_ref, arrived):
    width, hours = lay.width, lay.hours
    copies = [
        pltpu.make_async_copy(section_hbm, section_ref, arrived.at[0]),
        pltpu.make_async_copy(start_hbm, start_ref, arrived.at[1]),
        pltpu.make_async_copy(slab_hbm.at[:, lay.part(0)], slab_ref.at[:, lay.part(0)], arrived.at[2]),
    ]
    for copy in copies:
        copy.start()
    copies[0].wait()
    outgoing, incoming, inverse, keep, swap, diagonal = tables(section_ref, hours)
    later = lax.broadcasted_iota(jnp.int32, (hours, hours), 0)
    earlier = lax.broadcasted_iota(jnp.int32, (hours, hours), 1)
    columns = jnp.transpose(outgoing[:, :hours])
    full = outer(columns, inverse[:, :hours])
    full = jnp.where(later > earlier, full, jnp.where(later == earlier, diagonal, 0.0))
    copies[1].wait()
    start = start_ref[...]
    work[:width, lay.weights : lay.weights + hours] = exact_dot(start, full)
    work[width : width + STATES, lay.weights : lay.weights + hours] = incoming[:, :hours]
    handed = jnp.transpose(exact_dot(start, columns))
    handed = jnp.concatenate([handed, jnp.zeros((STATES, LANES - width), jnp.float32)], axis=1)
    table = work.at[:, lay.table : lay.table + LANES]
    table[STATES : 2 * STATES, :] = handed
    copies[2].wait()
    add_part(lay, 0, left, slab_ref, work, message_ref)
    for block in range(lay.blocks):
        work[:width, lay.filter_block(block)] = full[block * width : (block + 1) * width]
    for place, value in ((0, outgoing), (2, keep), (3, swap)):
        table[place * STATES : (place + 1) * STATES, :] = value


def head_kernel(lay, line, place_ref, section_hbm, slab_hbm, start_hbm, work, message_ref, *scratch):
    place = place_ref[0]

    @pl.when((place == 0) | (place == line - 1))
    def _():
        begin(lay, place < line // 2, section_hbm, slab_hbm, start_hbm, work, message_ref, *scratch)


def second_kernel(lay, line, place_ref, slab_hbm, _, work, message_ref, slab_ref, arrived):
    place = place_ref[0]

    @pl.when((place == 0) | (place == line - 1))
    def _():
        span = lay.part(1)
        copy = pltpu.make_async_copy(slab_hbm.at[:, span], slab_ref.at[:, span], arrived)
        copy.start()
        copy.wait()
        add_part(lay, 1, place < line // 2, slab_ref, work, message_ref)


def rest_kernel(lay, line, place_ref, section_hbm, slab_hbm, start_hbm, _, work, *refs):
    messages, scratch = refs[: lay.parts - 2], refs[lay.parts - 2 :]
    slab_ref, landed = scratch[0], scratch[-1]
    place = place_ref[0]
    left = place < line // 2
    inner = (place != 0) & (place != line - 1)
    copies = []
    for part in range(1, lay.parts):
        span = lay.part(part)
        copies.append(pltpu.make_async_copy(slab_hbm.at[:, span], slab_ref.at[:, span], landed.at[part - 1]))
        copies[-1].start()
    work[lay.enter, : lay.filter] = jnp.zeros((STATES, lay.filter), jnp.float32)

    @pl.when(inner)
    def _():
        begin(lay, left, section_hbm, slab_hbm, start_hbm, work, None, *scratch[:-1])

    copies[0].wait()

    @pl.when(inner)
    def _():
        add_part(lay, 1, left, slab_ref, work, None)

    for part in range(2, lay.parts):
        copies[part - 1].wait()
        add_part(lay, part, left, slab_ref, work, messages[part - 2])


def column_of(rows, width):
    return jnp.transpose(rows[:, :LANES])[:width]


def inward_kernel(lay, part, hop, line, place_ref, recv_ref, _, work, message_ref):
    width, span = lay.width, lay.part(part)
    place = place_ref[0]
    left = place == hop + 1

    @pl.when(left | (place == line - 2 - hop))
    def _():
        received, states = lay.take(recv_ref, part)
        states_own = work[lay.own, span]
        columns = column_of(jnp.where(left, lay.rows(work, 1), states[:, :LANES]), width)
        rows = jnp.where(left, states, states_own)
        total = received + work[:width, span] + outer(columns, rows)
        swap = lay.rows(work, 3)[:, 0:1]
        extra = advanced(states, lay.rows(work, 2)[:, 0:1], jnp.where(left, swap, -swap))
        extra = extra + jnp.where(left, states_own, lay.weights_row(work, part))
        lay.put(message_ref, total, extra)
        work[:width, span] = total
        work[lay.out, span] = extra
        work[lay.enter, span] = jnp.where(left, states, 0.0)


def middle_kernel(lay, part, line, place_ref, recv_ref, *refs):
    work, message_ref = refs[-2:]
    width, span = lay.width, lay.part(part)
    place = place_ref[0]
    left = place == line // 2 - 1

    @pl.when(left | (place == line // 2))
    def _():
        received, states = lay.take(recv_ref, part)
        handed = work[lay.out, span]
        columns = column_of(jnp.where(left, states[:, :LANES], handed[:, :LANES]), width)
        total = received + work[:width, span] + outer(columns, jnp.where(left, handed, states))
        extra = advanced(states, lay.rows(work, 2)[:, 0:1], lay.rows(work, 3)[:, 0:1]) + work[lay.own, span]
        lay.put(message_ref, total, extra)
        work[:width, span] = total

        @pl.when(jnp.logical_not(left))
        def _():
            work[lay.enter, span] = states


def outward_kernel(lay, part, hop, line, place_ref, recv_ref, _, work, message_ref):
    width, span = lay.width, lay.part(part)
    place = place_ref[0]
    right = place == line // 2 + 1 + hop

    @pl.when(right | (place == line // 2 - 2 - hop))
    def _():
        total, states = lay.take(recv_ref, part)
        extra = advanced(states, lay.rows(work, 2)[:, 0:1], lay.rows(work, 3)[:, 0:1]) + work[lay.own, span]
        lay.put(message_ref, total, extra)
        work[:width, span] = total

        @pl.when(right)
        def _():
            work[lay.enter, span] = states


def packed_shape(width, hours):
    return (width + width // 2, hours) if hours == 2 * width else (width, hours + width)


def packed(filtered, gram):
    width, hours = filtered.shape
    if hours == 2 * width:
        halves = jnp.concatenate([gram[: width // 2], gram[width // 2 :]], axis=1)
        return jnp.concatenate([filtered, halves], axis=0)
    return jnp.concatenate([filtered, gram], axis=1)


def unpacked(sums, width, hours):
    if hours == 2 * width:
        halves = sums[width:]
        return sums[:width], jnp.concatenate([halves[:, :width], halves[:, width:]], axis=0)
    return sums[:, :hours], sums[:, hours:]


def gather_kernel(lay, part, line, place_ref, slab_ref, recv_ref, _, work, *results):
    width, hours, span = lay.width, lay.hours, lay.part(part)
    place = place_ref[0]
    last_left, last_right = place == 0, place == line - 1
    outermost = (last_left | last_right) if line > 2 else False
    rounded = work[:width, span].astype(jnp.bfloat16)
    patterns = jnp.where(outermost, recv_ref[:, : lay.sizes[part]], rounded)
    states = work[lay.enter, span]
    if line > 2:
        states = jnp.where(last_right, lay.take(recv_ref, part)[1], states)

        own_left, own_right = span.start < lay.own_cells, span.stop > lay.own_cells * (line - 1)
        kept = (last_left if own_left else False) | (last_right if own_right else False)

        @pl.when(kept)
        def _():
            lost = work[:width, span] - rounded.astype(jnp.float32)
            work[:width, span] = patterns.astype(jnp.float32) + lost

    def product(value):
        return lax.dot_general(patterns, value, (((1,), (1,)), ((), ())), preferred_element_type=jnp.float32)

    blocks = (product(slab_ref[...]), product(patterns), product(doubled(states).astype(jnp.bfloat16)))
    sums = jnp.concatenate(blocks, axis=1)
    running = slice(lay.running, lay.running + hours + width + STATES)
    if part:
        sums = work[:width, running] + sums
    if part < lay.parts - 1:
        work[:width, running] = sums
        return
    (sums_ref,) = results
    filtered = [
        stacked_dot(sums[:, :hours], work[:width, lay.filter_block(block)], 1)
        for block in range(lay.blocks)
    ]
    filtered = filtered[0] if lay.blocks == 1 else jnp.concatenate(filtered, axis=1)
    entering = jnp.dot(sums[:, hours + width :], lay.rows(work, 0)[:, :hours], precision=TOP)
    sums_ref[...] = packed(filtered + entering, sums[:, hours : hours + width])


def own_kernel(lay, place_ref, work, owns_ref):
    start = pl.multiple_of(place_ref[0] * lay.own_cells, LANES)
    high, low = split(work[: lay.width, pl.ds(start, lay.own_cells)])
    owns_ref[...] = jnp.concatenate([high, low, high], axis=0)


def inverse_factor(gram):
    width = gram.shape[0]
    row = lax.broadcasted_iota(jnp.int32, (width, width), 0)
    column = lax.broadcasted_iota(jnp.int32, (width, width), 1)
    work = jnp.concatenate([gram, jnp.where(row == column, 1.0, 0.0)], axis=1)
    tiles = [work[place : place + STATES] for place in range(0, width, STATES)]
    done = []
    for first in range(0, width, STATES):
        block = first // STATES
        spread = [
            [jnp.broadcast_to(tile[:, first + q : first + q + 1], tile.shape) for q in range(STATES)]
            for tile in tiles[block:]
        ]
        rows = [tiles[block][q : q + 1] for q in range(STATES)]
        value = [[spread[0][q][p : p + 1] for q in range(p + 1)] for p in range(STATES)]
        for p in range(0, STATES, 2):
            one, two = rows[p], rows[p + 1]
            a, b, d = value[p][p], value[p + 1][p], value[p + 1][p + 1]
            over = 1.0 / (a * d - b * b)
            ratio = b / a
            done.append(one * lax.rsqrt(a))
            done.append((two - ratio * one) * lax.rsqrt(d - ratio * b))
            for q in range(p + 2, STATES):
                x, y = value[q][p], value[q][p + 1]
                first_part, second_part = (x * d - y * b) * over, (y * a - x * b) * over
                for t in range(p + 2, q + 1):
                    value[q][t] = value[q][t] - (first_part * value[t][p] + second_part * value[t][p + 1])
                rows[q] = rows[q] - (first_part * one + second_part * two)
                for low in spread[1:]:
                    low[q] = low[q] - (first_part * low[p] + second_part * low[p + 1])
            one, two = (d * one - b * two) * over, (a * two - b * one) * over
            for place, low in enumerate(spread[1:], block + 1):
                tiles[place] = tiles[place] - (low[p] * one + low[p + 1] * two)
    return jnp.concatenate(done, axis=0)[:, width:]


def tail_kernel(basis_scale, pcs_scale, *refs):
    *shares, owns_ref, basis_ref, pcs_ref = refs
    width = basis_ref.shape[1]
    shares = [share[...] for share in shares]
    while len(shares) > 1:
        shares = [one + two for one, two in zip(shares[::2], shares[1::2])]
    sums = shares[0]
    filtered, gram = unpacked(sums, width, pcs_ref.shape[1])
    inverse = inverse_factor(gram)
    pcs_ref[...] = stacked_dot(inverse * pcs_scale, filtered, 0)
    high, low = split(inverse * basis_scale)
    inverses = jnp.concatenate([high, high, low], axis=1)
    basis = jnp.dot(inverses, owns_ref[...], preferred_element_type=jnp.float32)
    for group in range(basis_ref.shape[0]):
        basis_ref[group] = basis[:, group * LANES : (group + 1) * LANES]


def call(kernel, name, out_shape, *args, scalars=1, far=0, scratch=(), in_place=0, final=False):
    smem, vmem = pl.BlockSpec(memory_space=pltpu.SMEM), pl.BlockSpec(memory_space=pltpu.VMEM)
    hbm = pl.BlockSpec(memory_space=pltpu.HBM)
    count = len(args)
    keep = pltpu.with_memory_space_constraint
    args = list(args[:scalars]) + [
        keep(arg, pltpu.HBM if place < far else pltpu.VMEM) for place, arg in enumerate(args[scalars:])
    ]
    return pl.pallas_call(
        kernel,
        out_shape=out_shape if final else [pltpu.VMEM(out.shape, out.dtype) for out in out_shape],
        in_specs=[smem] * scalars + [hbm] * far + [vmem] * (count - scalars - far),
        out_specs=[vmem] * len(out_shape),
        scratch_shapes=scratch,
        input_output_aliases={count - in_place + place: place for place in range(in_place)},
        compiler_params=pltpu.CompilerParams(vmem_limit_bytes=VMEM_LIMIT),
        cost_estimate=pl.CostEstimate(flops=1, bytes_accessed=1, transcendentals=0),
        name=name,
    )(*args)


def complete(moves, size, cores, both):
    moves = moves + [(target, source) for source, target in moves] if both else moves
    used = {device for move in moves for device in move}
    full = [(source * cores + core, target * cores + core) for source, target in moves for core in range(cores)]
    other = 1 if cores % 2 == 0 else 0
    idle = [device * cores + core for device in range(size) if device not in used for core in range(cores)]
    return full + [(device, device ^ other) for device in idle]


def local(slab, start, sections):
    hours, cells = slab.shape
    width = start.shape[1]
    line = lax.axis_size("tm")
    half = line // 2
    groups, parts = cells // LANES, len(SIZES)
    ends = [groups * sum(SIZES[:part]) // sum(SIZES) * LANES for part in range(parts + 1)]
    sizes = [end - start for start, end in zip(ends, ends[1:])]
    lay = Layout(hours, cells, width, sizes, line)
    f32, bf16 = jnp.float32, jnp.bfloat16
    shape = jax.ShapeDtypeStruct
    place = lax.axis_index("tm").astype(jnp.int32).reshape(1)
    work_shape = shape(lay.shape, f32)

    def message_shape(room):
        return shape((width, room + lay.extra), bf16)

    def room(exchange):
        held = [part for part in (exchange, exchange - LAG) if 0 <= part < parts]
        return max(sizes[part] for part in held[: 2 if half == 2 else 1])

    first, *others = [message_shape(room(part)) for part in range(parts)]
    scratch = [
        pltpu.VMEM(slab.shape, bf16), pltpu.VMEM((width, hours), bf16), pltpu.SMEM((2, 3), f32), pltpu.SemaphoreType.DMA((3,)),
    ]
    inputs = (place, sections.T, slab, start.T)
    work, message = call(
        functools.partial(head_kernel, lay, line), "head", [work_shape, first], *inputs, far=3, scratch=scratch
    )
    work, second = call(
        functools.partial(second_kernel, lay, line), "second", [work_shape, others[0]], place, slab, work, far=1,
        in_place=1, scratch=[pltpu.VMEM(slab.shape, bf16), pltpu.SemaphoreType.DMA(())],
    )
    work, *messages = call(
        functools.partial(rest_kernel, lay, line), "rest", [work_shape] + others[1:], *inputs, work,
        far=3, in_place=1, scratch=[*scratch, pltpu.SemaphoreType.DMA((parts - 1,))],
    )
    messages = [message, second, *messages]

    def results(part, exchange=None):
        return [work_shape, message_shape(sizes[part] if exchange is None else room(exchange))]

    def inward_moves(hop):
        return [(hop, hop + 1), (line - 1 - hop, line - 2 - hop)]

    def send(message, moves, both=False):
        return lax.ppermute(message, ("tm", "lon"), complete(moves, line, lax.axis_size("lon"), both))

    def gather(part, block, work):
        shapes = [work_shape]
        if part == parts - 1:
            shapes += [shape(packed_shape(width, hours), f32)]
        kernel = functools.partial(gather_kernel, lay, part, line)
        return call(kernel, "gather", shapes, place, slab[:, lay.part(part)], block, work, in_place=1)

    def inward(part, hop, block, work):
        kernel = functools.partial(inward_kernel, lay, part, hop, line)
        return call(kernel, "inward", results(part), place, block, work, in_place=1)

    def middle(part, block, work, *message, exchange=None):
        kernel = functools.partial(middle_kernel, lay, part, line)
        return call(kernel, "middle", results(part, exchange), place, block, work, *message, in_place=1 + len(message))

    middle_moves = [(half - 1, half), (half, half - 1)]
    if half == 2:
        crossing = [send(message, inward_moves(0), True) for message in messages[:LAG]]
        between = [None] * parts
        for step in range(parts + LAG):
            if step < parts:
                work, message = inward(step, 0, crossing[step], work)
                between[step] = send(message, middle_moves)
            if step >= LAG:
                work, *rest = gather(step - LAG, crossing[step], work)
            if 1 <= step <= parts:
                later = step - 1 + LAG
                swapped_in = [messages[later]] if later < parts else []
                work, message = middle(step - 1, between[step - 1], work, *swapped_in, exchange=later)
                crossing.append(send(message, inward_moves(0), True))
    else:
        arriving = [send(message, inward_moves(0)) if half > 1 else message for message in messages]
        for part in range(parts):
            message, block = messages[part], arriving[part]
            for hop in range(half - 1):
                work, message = inward(part, hop, block, work)
                if hop < half - 2:
                    block = send(message, inward_moves(hop + 1))
            block = send(message, middle_moves)
            work, message = middle(part, block, work)
            for hop in range(half - 1):
                block = send(message, [(target, source) for source, target in inward_moves(half - 2 - hop)])
                if hop < half - 2:
                    kernel = functools.partial(outward_kernel, lay, part, hop, line)
                    work, message = call(kernel, "outward", results(part), place, block, work, in_place=1)
            work, *rest = gather(part, block, work)
    (running,) = rest
    kernel = functools.partial(own_kernel, lay)
    (owns,) = call(kernel, "own", [shape((3 * width, lay.own_cells), bf16)], place, work)

    cores, bands = lax.axis_size("lon"), lax.axis_size("lat")
    stride = 1
    while stride < cores:
        running = running + lax.ppermute(running, "lon", [(i, i ^ stride) for i in range(cores)])
        stride *= 2
    shares = [running]
    shares += [lax.ppermute(running, "lat", [(i, i ^ way) for i in range(bands)]) for way in range(1, bands)]

    cells_all = cells * lax.axis_size("lat") * lax.axis_size("lon")
    basis, pcs = call(
        functools.partial(tail_kernel, math.sqrt(cells_all), math.sqrt(hours * line / cells_all)), "tail",
        [shape((lay.own_cells // LANES, width, LANES), f32), shape((width, hours), f32)],
        *shares, owns, scalars=0, final=True,
    )
    return (basis, pcs.T)


def solution(mesh):
    return jax.shard_map(
        local,
        mesh=mesh,
        in_specs=(P("tm", ("lat", "lon")), P("tm", None), P()),
        out_specs=(P(("lat", "lon", "tm"), None, None), P("tm", None)),
        check_vma=False,
    )
```
